32 devices in a mesh: fsdp: 4 (over z), ctx: 2 (over core), tp: 4 (over y, x).
Axes of the slice: x: 2, y: 2, z: 4, core: 2. Of those that a mesh axis runs over, the one named last changes fastest.
Arguments:
- tokens: bfloat16 [8, 2048, 1024], P('fsdp', 'ctx', 'tp'), may hold values from -6 to 6
- lengths: int32 [8], P('fsdp'), may hold values from 512 to 2048, as said below
- w_query: bfloat16 [1024, 1024], P('fsdp', 'tp'), may hold values from -0.1875 to 0.1875
- w_keyval: bfloat16 [1024, 256], P('fsdp'), may hold values from -0.1875 to 0.1875
- w_out: bfloat16 [1024, 1024], P('tp', 'fsdp'), may hold values from -3 to 3
- w_gateup: bfloat16 [2, 1024, 3072], P(None, 'fsdp', 'tp'), may hold values from -0.1875 to 0.1875
- w_down: bfloat16 [3072, 1024], P('tp', 'fsdp'), may hold values from -0.109375 to 0.109375
- gain_attn: bfloat16 [1024], P('tp'), may hold values from 0.5 to 1.5
- gain_mlp: bfloat16 [1024], P('tp'), may hold values from 0.5 to 1.5
- cotangent: bfloat16 [8, 2048, 1024], P('fsdp', 'ctx', 'tp'), may hold values from -6 to 6
Outputs:
- outputs: bfloat16 [8, 2048, 1024], P('fsdp', 'ctx', 'tp')
- grad_tokens: float32 [8, 2048, 1024], P('fsdp', 'ctx', 'tp')
- grad_query: float32 [1024, 1024], P(('fsdp', 'ctx'), 'tp')
- grad_keyval: float32 [1024, 256], P(('fsdp', 'ctx'))
- grad_output_proj: float32 [1024, 1024], P('tp', ('fsdp', 'ctx'))
- grad_gateup: float32 [2, 1024, 3072], P(None, ('fsdp', 'ctx'), 'tp')
- grad_down: float32 [3072, 1024], P('tp', ('fsdp', 'ctx'))
- grad_gain_attn: float32 [1024], P('tp')
- grad_gain_mlp: float32 [1024], P('tp')
The draws below stay inside these ranges and needn't reach their ends.
Inputs may be any that keep to these rules, and one draw needn't show every extreme that they name: `lengths`: in every aligned block of 2 slots one slot has 1536 valid tokens or more; some slot has exactly 2048 and some exactly 512.
All inputs are finite; a program needn't handle non-finite values.
Results may differ from the reference program's by a relative error of at most 0.015.
Values may be sent and summed in bfloat16 or wider, within the bound.
No kernel may reach another device: no remote copies, remote signals or barrier semaphores. Data moves between devices by JAX's collectives and lax.ppermute only.
A program may use at most 128 MiB of HBM per device.

```python
import jax
import jax.numpy as jnp
from jax import lax

D = 1024
HEADS = 8
HEAD = 128
FF = 3072
WINDOW = 1024
SLOTS_DEV = 2
LEN = 2048
SLOTS = 8


def draw_lengths(key, part):
    key_base, key_long, key_pick, key_top, key_low = jax.random.split(key, 5)
    slot_ids = jnp.arange(SLOTS, dtype=jnp.int32)
    groups = SLOTS // SLOTS_DEV
    base_lengths = jax.random.randint(key_base, (SLOTS,), WINDOW // 2, LEN + 1)
    long_lengths = jax.random.randint(key_long, (SLOTS,), LEN - WINDOW // 2, LEN + 1)
    picked = jax.random.randint(key_pick, (groups,), 0, SLOTS_DEV)
    chosen = slot_ids % SLOTS_DEV == jnp.repeat(picked, SLOTS_DEV)
    result = jnp.where(chosen, long_lengths, base_lengths)
    top_group = jax.random.randint(key_top, (), 0, groups)
    low_group = jax.random.randint(key_low, (), 0, groups)
    top_slot = top_group * SLOTS_DEV + picked[top_group]
    low_slot = low_group * SLOTS_DEV + (picked[low_group] + 1) % SLOTS_DEV
    result = jnp.where(slot_ids == top_slot, LEN, result)
    result = jnp.where(slot_ids == low_slot, WINDOW // 2, result)
    return result.astype(jnp.int32)


def block_scale(stream_key, extent, pieces, low, high):
    def one(axis_at, blocks):
        steps = jax.random.uniform(jax.random.fold_in(jax.random.fold_in(stream_key, 6), axis_at), (blocks,), jnp.float32, low / len(pieces), high / len(pieces))
        return jnp.repeat(jnp.exp(steps), extent[axis_at] // blocks).reshape((-1,) + (1,) * (len(extent) - axis_at - 1))

    loudness = one(*pieces[0])
    for cut in pieces[1:]:
        loudness = loudness * one(*cut)
    return loudness


def normal_values(key, dims, spread, reach, pieces=(), kind=jnp.bfloat16):
    entries = spread * jax.random.normal(key, dims, jnp.float32)
    if pieces:
        entries = entries * block_scale(key, dims, pieces, -0.22, 0.18)
    return jnp.clip(entries, -reach, reach).astype(kind)


def setup_inputs(seed: int = 0) -> dict:
    arg_keys = jax.random.split(jax.random.key(seed), 11)
    return {
        "tokens": normal_values(arg_keys[0], (SLOTS, LEN, D), 1.0, 6.0, ((0, 4), (1, 2), (2, 4))),
        "lengths": draw_lengths(jax.random.fold_in(arg_keys[10], 71), 0),
        "w_query": normal_values(arg_keys[2], (D, HEADS * HEAD), D ** -0.5, 0.1875, ((0, 4), (1, 4))),
        "w_keyval": normal_values(arg_keys[3], (D, 2 * HEAD), D ** -0.5, 0.1875, ((0, 4),)),
        "w_out": normal_values(arg_keys[4], (HEADS * HEAD, D), (4 * HEADS * HEAD // WINDOW) ** -0.5, 3.0, ((0, 4), (1, 4))),
        "w_gateup": normal_values(arg_keys[5], (2, D, FF), D ** -0.5, 0.1875, ((1, 4), (2, 4))),
        "w_down": normal_values(arg_keys[6], (FF, D), FF ** -0.5, 0.109375, ((0, 4), (1, 4))),
        "gain_attn": jnp.clip(1.0 + 0.1 * jax.random.normal(arg_keys[7], (D,), jnp.float32), 0.5, 1.5).astype(jnp.bfloat16),
        "gain_mlp": jnp.clip(1.0 + 0.1 * jax.random.normal(arg_keys[8], (D,), jnp.float32), 0.5, 1.5).astype(jnp.bfloat16),
        "cotangent": normal_values(arg_keys[9], (SLOTS, LEN, D), 1.0, 6.0, ((0, 4), (1, 2), (2, 4))),
    }


epsilon = 1e-06
highest = lax.Precision.HIGHEST

@jax.custom_vjp
def low(v):
    return lax.optimization_barrier(v.astype(jnp.bfloat16)).astype(jnp.float32)

@jax.custom_vjp
def low_back(v):
    return v

def low_keep(v):
    return (low(v), None)

def low_pass(kept, grad):
    return (grad,)

def back_keep(v):
    return (v, None)

def back_low(kept, grad):
    return (low(grad),)
low.defvjp(low_keep, low_pass)
low_back.defvjp(back_keep, back_low)

def rotary(vectors, positions, direction):
    half_width = vectors.shape[-1] // 2
    freq_table = 10000.0 ** (-jnp.arange(half_width, dtype=jnp.float32) / half_width)
    angles = positions.astype(jnp.float32)[:, None] * freq_table[None, :]
    cosine = jnp.cos(angles)[:, None, :]
    sine_part = direction * jnp.sin(angles)[:, None, :]
    leading = vectors[..., :half_width]
    trailing = vectors[..., half_width:]
    return jnp.concatenate([leading * cosine - trailing * sine_part, trailing * cosine + leading * sine_part], axis=-1)

def rms_norm(values, gain_vec):
    return values * lax.rsqrt(lax.optimization_barrier(jnp.mean(values * values, axis=-1, keepdims=True)) + epsilon) * gain_vec

def attend(queries, key_rows, value_rows, length):
    row_count = queries.shape[0]
    block_rows = min(512, row_count)
    score_scale = HEAD ** (-0.5)
    key_pos = jnp.arange(row_count, dtype=jnp.int32)

    def one_block(block_index):
        row_start = (block_index * block_rows).astype(jnp.int32)
        block_query = lax.dynamic_slice_in_dim(queries, row_start, block_rows, 0)
        query_pos = row_start + jnp.arange(block_rows, dtype=jnp.int32)
        scores = low_back(jnp.einsum('rhe,se->rhs', block_query, key_rows, precision=highest) * score_scale)
        allowed = (key_pos[None, :] <= query_pos[:, None]) & (key_pos[None, :] > query_pos[:, None] - WINDOW) & (key_pos[None, :] < length) | (key_pos[None, :] == query_pos[:, None])
        scores = jnp.where(allowed[:, None, :], scores, -1e+30)
        soft_weights = low(jax.nn.softmax(scores, axis=-1))
        return jnp.einsum('rhs,se->rhe', soft_weights, value_rows, precision=highest)
    blocks = lax.map(jax.checkpoint(one_block), jnp.arange(row_count // block_rows, dtype=jnp.int32))
    return blocks.reshape(row_count, -1)

def block_forward(inputs, weights, length):
    w_query, w_keyval, w_out, w_gateup, w_down, gain_attn, gain_mlp = weights
    row_count = inputs.shape[0]
    positions = jnp.arange(row_count, dtype=jnp.int32)
    normed = low(rms_norm(inputs, gain_attn))
    query_lin = low_back(jnp.dot(normed, w_query, precision=highest))
    keyval_lin = low_back(jnp.dot(normed, w_keyval, precision=highest))
    queries = low(rotary(query_lin.reshape(row_count, HEADS, HEAD), positions, 1.0))
    key_rows = low(rotary(keyval_lin[:, None, :HEAD], positions, 1.0)[:, 0])
    value_rows = low(keyval_lin[:, HEAD:])
    mixed_heads = low(low_back(attend(queries, key_rows, value_rows, length)))
    branch = low_back(jnp.dot(mixed_heads, w_out, precision=highest))
    hidden = inputs + branch
    normed_mlp = low(rms_norm(hidden, gain_mlp))
    gate_proj = low_back(jnp.dot(normed_mlp, w_gateup[0], precision=highest))
    up_proj = low_back(jnp.dot(normed_mlp, w_gateup[1], precision=highest))
    active = low(jax.nn.gelu(gate_proj, approximate=True) * up_proj)
    return hidden + low_back(jnp.dot(active, w_down, precision=highest))

def reference(tokens, lengths, w_query, w_keyval, w_out, w_gateup, w_down, gain_attn, gain_mlp, cotangent):
    weights = tuple((weight.astype(jnp.float32) for weight in (w_query, w_keyval, w_out, w_gateup, w_down, gain_attn, gain_mlp)))
    zero_grads = jax.tree.map(jnp.zeros_like, weights)

    def per_slot(totals, slot_data):
        inputs, cot_rows, length = slot_data
        outputs, pullback = jax.vjp(lambda row_block, params: block_forward(row_block, params, length), inputs.astype(jnp.float32), weights)
        valid_rows = (jnp.arange(inputs.shape[0], dtype=jnp.int32) < length)[:, None]
        grad_rows, grad_weights = pullback(jnp.where(valid_rows, cot_rows.astype(jnp.float32), 0.0))
        return (jax.tree.map(jnp.add, totals, grad_weights), (outputs.astype(jnp.bfloat16), grad_rows))
    totals, (outputs, grad_tokens) = lax.scan(per_slot, zero_grads, (tokens, cotangent, lengths))
    return (outputs, grad_tokens, totals[0], totals[1], totals[2], totals[3], totals[4], totals[5], totals[6])
```

```python
import functools
import math

import jax
import jax.numpy as jnp
from jax import lax
from jax.experimental import pallas as pl
from jax.experimental.pallas import tpu as pltpu
from jax.sharding import Mesh
from jax.sharding import PartitionSpec as P

D = 1024
HEAD = 128
WINDOW = 1024
ROWS = 256
EPSILON = 1e-06
NEG = -1e30
LOG2E = math.log2(math.e)
BF = jnp.bfloat16
F32 = jnp.float32


def mm(a, b):
    return jnp.dot(a, b, preferred_element_type=F32)


def mm_nt(a, b):
    return lax.dot_general(a, b, (((1,), (1,)), ((), ())), preferred_element_type=F32)


def mm_tn(a, b):
    return lax.dot_general(a, b, (((0,), (0,)), ((), ())), preferred_element_type=F32)


def key_bias(step, start, length):
    span = WINDOW + ROWS
    row = lax.broadcasted_iota(jnp.int32, (ROWS, span), 0)
    col = lax.broadcasted_iota(jnp.int32, (ROWS, span), 1)
    pos = start - WINDOW + step * ROWS + col
    ahead = col - row - WINDOW
    inside = (ahead <= 0) & (ahead > -WINDOW) & (pos >= 0) & (pos < length)
    return jnp.where(inside | (ahead == 0), 0.0, NEG).astype(F32)


def attend_kernel(heads, where_ref, q_ref, kv_ref, mixed_ref, lse_ref, bias_ref):
    step = pl.program_id(0)
    span = WINDOW + ROWS
    bias_ref[...] = key_bias(step, where_ref[0], where_ref[1])
    keys = kv_ref[pl.ds(step * ROWS, span), :HEAD]
    values = kv_ref[pl.ds(step * ROWS, span), HEAD:]
    for h in range(heads):
        cols = slice(h * HEAD, (h + 1) * HEAD)
        s = mm_nt(q_ref[:, cols], keys) * (HEAD**-0.5 * LOG2E) + bias_ref[...]
        top = jnp.max(s, axis=1, keepdims=True)
        p = jnp.exp2(s - top)
        total = jnp.sum(p, axis=1, keepdims=True)
        mixed = mm(p.astype(BF), values) / total
        mixed_ref[:, cols] = mixed.astype(BF)
        lse_ref[:, h : h + 1] = top + jnp.log2(total)


def attend(q, kv, where):
    rows, width = q.shape
    heads = width // HEAD
    steps = rows // ROWS
    return pl.pallas_call(
        functools.partial(attend_kernel, heads),
        grid_spec=pltpu.PrefetchScalarGridSpec(
            num_scalar_prefetch=1,
            grid=(steps,),
            in_specs=[
                pl.BlockSpec((ROWS, width), lambda i, w: (i, 0)),
                pl.BlockSpec(kv.shape, lambda i, w: (0, 0)),
            ],
            out_specs=[
                pl.BlockSpec((ROWS, width), lambda i, w: (i, 0)),
                pl.BlockSpec((ROWS, heads), lambda i, w: (i, 0)),
            ],
            scratch_shapes=[pltpu.VMEM((ROWS, WINDOW + ROWS), F32)],
        ),
        out_shape=[
            jax.ShapeDtypeStruct((rows, width), BF),
            jax.ShapeDtypeStruct((rows, heads), F32),
        ],
        compiler_params=pltpu.CompilerParams(vmem_limit_bytes=40 << 20),
        cost_estimate=pl.CostEstimate(
            flops=4 * rows * width * (WINDOW + ROWS),
            bytes_accessed=2 * q.size * 2 + kv.size * 2,
            transcendentals=rows * heads * (WINDOW + ROWS),
        ),
        name="attend",
    )(where, q, kv)


def attend_back_kernel(
    heads, where_ref, q_ref, kv_ref, mixed_ref, lse_ref, gm_ref, gq_ref, gkv_ref, bias_ref
):
    step = pl.program_id(0)
    span = WINDOW + ROWS
    scale = HEAD**-0.5

    @pl.when(step == 0)
    def _():
        gkv_ref[...] = jnp.zeros_like(gkv_ref)

    bias_ref[...] = key_bias(step, where_ref[0], where_ref[1])
    here = pl.ds(step * ROWS, span)
    keys = kv_ref[here, :HEAD]
    values = kv_ref[here, HEAD:]
    for h in range(heads):
        cols = slice(h * HEAD, (h + 1) * HEAD)
        q = q_ref[:, cols]
        gm = gm_ref[:, cols]
        s = mm_nt(q, keys) * (scale * LOG2E) + bias_ref[...]
        p = jnp.exp2(s - lse_ref[:, h : h + 1])
        gp = mm_nt(gm, values)
        inner = jnp.sum(
            gm.astype(F32) * mixed_ref[:, cols].astype(F32), axis=1, keepdims=True
        )
        gs = (p * (gp - inner)).astype(BF)
        gq_ref[:, cols] = mm(gs, keys) * scale
        gkv_ref[here, :HEAD] += mm_tn(gs, q) * scale
        gkv_ref[here, HEAD:] += mm_tn(p.astype(BF), gm)


def attend_back(q, kv, mixed, lse, grad_mixed, where):
    rows, width = q.shape
    heads = width // HEAD
    steps = rows // ROWS
    block = pl.BlockSpec((ROWS, width), lambda i, w: (i, 0))
    whole = pl.BlockSpec(kv.shape, lambda i, w: (0, 0))
    return pl.pallas_call(
        functools.partial(attend_back_kernel, heads),
        grid_spec=pltpu.PrefetchScalarGridSpec(
            num_scalar_prefetch=1,
            grid=(steps,),
            in_specs=[
                block,
                whole,
                block,
                pl.BlockSpec((ROWS, heads), lambda i, w: (i, 0)),
                block,
            ],
            out_specs=[block, whole],
            scratch_shapes=[pltpu.VMEM((ROWS, WINDOW + ROWS), F32)],
        ),
        out_shape=[
            jax.ShapeDtypeStruct((rows, width), F32),
            jax.ShapeDtypeStruct(kv.shape, F32),
        ],
        compiler_params=pltpu.CompilerParams(vmem_limit_bytes=40 << 20),
        cost_estimate=pl.CostEstimate(
            flops=10 * rows * width * (WINDOW + ROWS),
            bytes_accessed=5 * q.size * 2 + kv.size * 6,
            transcendentals=rows * heads * (WINDOW + ROWS),
        ),
        name="attend_back",
    )(where, q, kv, mixed, lse, grad_mixed)


def swap(value, axis):
    return lax.ppermute(value, axis, [(0, 1), (1, 0)])


def swap_both(value):
    return lax.ppermute(value, ("ty", "tx"), [(i, i ^ 3) for i in range(4)])


def pick(flag, ones, zeros):
    return jnp.where(flag == 1, ones, zeros)


def pair(flag, own, other, axis):
    return jnp.concatenate([pick(flag, other, own), pick(flag, own, other)], axis=axis)


def half_at(value, index, axis):
    size = value.shape[axis] // 2
    return lax.dynamic_slice_in_dim(value, index * size, size, axis)


def along_fsdp(blocks, index):
    count = blocks.shape[0]
    total = lax.dynamic_index_in_dim(blocks, index, 0, False).astype(F32)
    if count > 4:
        return lax.psum_scatter(blocks, "fsdp", scatter_dimension=0, tiled=False).astype(F32)
    for step in range(1, count):
        block = lax.dynamic_index_in_dim(blocks, (index + step) % count, 0, False)
        came = lax.ppermute(block, "fsdp", [(i, (i + step) % count) for i in range(count)])
        total = total + came.astype(F32)
    return total


def body(
    tokens, lengths, w_query, w_keyval, w_out, w_gateup, w_down, gain_attn, gain_mlp, cotangent
):
    shards = lax.axis_size("fsdp")
    z, c = lax.axis_index("fsdp"), lax.axis_index("ctx")
    y, x = lax.axis_index("ty"), lax.axis_index("tx")
    seq_rows = tokens.shape[1]
    rows = seq_rows // 2
    feats = tokens.shape[2]
    depth = w_query.shape[0]
    sub = depth // 2
    eighth = depth // 8
    length = lax.dynamic_index_in_dim(lengths, y, 0, False)
    row_start = c * seq_rows + x * rows
    where = jnp.stack([row_start, length]).astype(jnp.int32)

    keyval_part = lax.dynamic_slice_in_dim(w_keyval, ((c * 2 + y) * 2 + x) * eighth, eighth, 0)
    qkv_part = jnp.concatenate([half_at(w_query, c, 0), keyval_part], axis=0)
    qkv_all = lax.all_gather(qkv_part, ("ty", "tx", "fsdp", "ctx"), axis=0, tiled=False)
    qkv_all = qkv_all.reshape(4, shards, 2, sub + eighth, feats)
    w_q = qkv_all[:, :, :, :sub].reshape(4, D, feats)
    w_q = w_q.transpose(1, 0, 2).reshape(D, 4 * feats)
    w_kv = qkv_all[:, :, :, sub:].transpose(1, 2, 0, 3, 4).reshape(D, feats)

    out_part = half_at(w_out, c, 0)
    out_all = lax.all_gather(out_part, ("ty", "tx", "ctx", "fsdp"), axis=0, tiled=False)
    w_o = out_all.reshape(8, shards, -1, depth).transpose(0, 2, 1, 3).reshape(-1, D)

    units = w_gateup.shape[2] // 2
    gateup_part = half_at(w_gateup, c, 2)
    down_part = half_at(w_down, c, 0)
    mlp_part = jnp.concatenate([gateup_part[0], gateup_part[1], down_part.T], axis=1)
    w_mlp = lax.all_gather(mlp_part, ("tx", "fsdp"), axis=0, tiled=False)
    w_mlp = w_mlp.reshape(2, D, 3 * units)

    gains = jnp.stack([gain_attn, gain_mlp])

    def piece(slot, half):
        block = lax.dynamic_index_in_dim(tokens, slot, 0, False)
        block = half_at(block, half, 0)
        return jnp.concatenate([block, gains, jnp.zeros((14, feats), BF)], axis=0)

    across_x = swap(piece(y, 1 - x), "tx")
    across_y = swap(piece(1 - y, x), "ty")
    across_both = swap_both(piece(1 - y, 1 - x))
    mine = piece(y, x)
    full = pair(
        y, pair(x, mine, across_x, 1), pair(x, across_y, across_both, 1), 1
    )
    resid = full[:rows].astype(F32)
    gain_a = full[rows].astype(F32)
    gain_m = full[rows + 1].astype(F32)

    t_local = c * seq_rows + jnp.arange(seq_rows, dtype=jnp.int32)
    cot = jnp.where((t_local[None, :] < lengths[:, None])[:, :, None], cotangent, 0)
    cot_x = swap(half_at(cot, 1 - x, 1), "tx")
    cot_pair = pair(x, half_at(cot, x, 1), cot_x, 2)
    cot_other = swap(cot_pair, "ty")
    cot_full = pair(y, cot_pair, cot_other, 2)
    cot_full = jnp.concatenate([pick(y, cot_full[1], cot_full[0]), pick(y, cot_full[0], cot_full[1])], axis=0)
    grad_rows = jnp.concatenate([cot_full, swap(cot_full, "ctx")], axis=0)
    grad_final = cot_full[:rows].astype(F32)

    inv_attn = lax.rsqrt(jnp.mean(resid * resid, axis=1, keepdims=True) + EPSILON)
    hat_attn = resid * inv_attn
    normed_attn = (hat_attn * gain_a).astype(BF)

    half_width = HEAD // 2
    freq = 10000.0 ** (-jnp.arange(half_width, dtype=F32) / half_width)
    angles = (row_start + jnp.arange(rows, dtype=jnp.int32)).astype(F32)[:, None] * freq[None, :]
    cosine, sine = jnp.cos(angles), jnp.sin(angles)
    cos_full = jnp.concatenate([cosine, cosine], axis=1)[:, None, :]
    sin_full = jnp.concatenate([-sine, sine], axis=1)[:, None, :]

    def rotate(value, direction):
        value = value.reshape(rows, -1, HEAD)
        turned = jnp.concatenate([value[..., half_width:], value[..., :half_width]], axis=2)
        return (value * cos_full + turned * (direction * sin_full)).reshape(rows, -1)

    q = rotate(mm(normed_attn, w_q), 1.0).astype(BF)
    keyval_lin = mm(normed_attn, w_kv)
    kv_own = jnp.concatenate([rotate(keyval_lin[:, :HEAD], 1.0), keyval_lin[:, HEAD:]], axis=1)
    kv_own = kv_own.astype(BF)
    kv_x = swap(kv_own, "tx")
    kv_c = swap(jnp.concatenate([kv_own, kv_x], axis=1), "ctx")
    kv_all = jnp.concatenate(
        [kv_c[:, :feats], pick(x, kv_x, kv_c[:, feats:]), kv_own], axis=0
    )
    mixed, lse = attend(q, kv_all, where)
    hidden = resid + mm(mixed, w_o)

    inv_mlp = lax.rsqrt(jnp.mean(hidden * hidden, axis=1, keepdims=True) + EPSILON)
    hat_mlp = hidden * inv_mlp
    normed_mlp = (hat_mlp * gain_m).astype(BF)
    two = jnp.concatenate([normed_mlp, swap(normed_mlp, "ty")], axis=0)
    mlp_rows = jnp.concatenate([two, swap(two, "ctx")], axis=0)

    grad_normed = 0.0
    branch = 0.0
    grad_parts = []
    for part in range(2):
        w_gu = w_mlp[part, :, : 2 * units]
        w_dt = w_mlp[part, :, 2 * units :]
        lin = mm(mlp_rows, w_gu)
        gate, up = lin[:, :units], lin[:, units:]
        grad_active = mm(grad_rows, w_dt)
        inner = math.sqrt(2 / math.pi) * (gate + 0.044715 * gate * gate * gate)
        tanh = jnp.tanh(inner)
        gelu = 0.5 * gate * (1.0 + tanh)
        slope = 0.5 * (1.0 + tanh) + 0.5 * gate * (1.0 - tanh * tanh) * math.sqrt(
            2 / math.pi
        ) * (1.0 + 3 * 0.044715 * gate * gate)
        active = (gelu * up).astype(BF)
        grad_gu = jnp.concatenate(
            [(grad_active * up * slope).astype(BF), (grad_active * gelu).astype(BF)], axis=1
        )
        grad_normed = grad_normed + mm_nt(grad_gu, w_gu)
        branch = branch + mm_nt(active, w_dt)
        grad_parts.append(
            jnp.concatenate(
                [mm_tn(mlp_rows, grad_gu).astype(BF), mm_tn(grad_rows, active).astype(BF)], axis=1
            )
        )

    group = 2 * rows
    grad_normed = grad_normed.astype(BF)
    grad_normed = grad_normed[:group].astype(F32) + swap(grad_normed[group:], "ctx").astype(F32)
    grad_normed = grad_normed[:rows] + swap(grad_normed[rows:].astype(BF), "ty").astype(F32)

    branch = branch.astype(BF)
    partial = branch[:group].astype(F32) + swap(branch[group:], "ctx").astype(F32)
    partial = partial.reshape(2, rows, D)
    partial = jnp.stack([partial[0] + hidden, partial[1]]).astype(BF)
    came = swap(half_at(partial, 1 - y, 2), "ty")
    summed = half_at(partial, y, 2).astype(F32) + came[::-1].astype(F32)
    summed = summed.astype(BF)
    summed = jnp.stack([pick(y, summed[1], summed[0]), pick(y, summed[0], summed[1])])
    outputs = pair(x, half_at(summed, x, 2), swap(half_at(summed, 1 - x, 2), "tx"), 1)

    mlp_grads = jnp.stack(grad_parts).reshape(2 * shards, depth, 3 * units)
    mlp_grads = lax.psum_scatter(mlp_grads, ("tx", "fsdp"), scatter_dimension=0, tiled=False)
    mlp_other = swap(half_at(mlp_grads, 1 - c, 0), "ctx")
    mlp_own = half_at(mlp_grads, c, 0)

    def units_of(at):
        cut = slice(at * units, (at + 1) * units)
        return pair(c, mlp_own[:, cut], mlp_other[:, cut], 1).astype(F32)

    grad_gateup = jnp.stack([units_of(0), units_of(1)])
    grad_down = units_of(2).T

    def norm_back(grad, hat, inv, gain):
        g = grad * gain
        dots = jnp.mean(g * hat, axis=1, keepdims=True)
        return inv * (g - hat * dots), jnp.sum(grad * hat, axis=0)

    back, grad_gain_mlp = norm_back(grad_normed, hat_mlp, inv_mlp, gain_m)
    grad_hidden = grad_final + back
    grad_hidden_low = grad_hidden.astype(BF)
    grad_mixed = mm_nt(grad_hidden_low, w_o).astype(BF)
    grad_wout = mm_tn(mixed, grad_hidden_low).astype(BF)
    grad_wout = grad_wout.reshape(4, -1, shards, 2, sub).transpose(0, 2, 3, 1, 4)
    grad_wout = grad_wout.reshape((-1,) + grad_wout.shape[3:])
    grad_output_proj = lax.psum_scatter(
        grad_wout, ("ty", "tx", "fsdp", "ctx"), scatter_dimension=0, tiled=False
    ).astype(F32)

    grad_q, grad_kv = attend_back(q, kv_all, mixed, lse, grad_mixed, where)
    kv_far, kv_near, kv_here = grad_kv[:rows], grad_kv[rows : 2 * rows], grad_kv[2 * rows :]
    near = swap(kv_near.astype(BF), "tx").astype(F32)
    sent = swap((kv_far + pick(x, near, 0.0)).astype(BF), "ctx").astype(F32)
    grad_kv = kv_here + pick(x, 0.0, near) + sent
    grad_kv_lin = jnp.concatenate(
        [rotate(grad_kv[:, :HEAD], -1.0), grad_kv[:, HEAD:]], axis=1
    ).astype(BF)
    grad_q_lin = rotate(grad_q, -1.0).astype(BF)
    grad_wq = mm_tn(normed_attn, grad_q_lin).astype(BF)
    grad_wkv = mm_tn(normed_attn, grad_kv_lin).astype(BF)
    grad_normed_a = mm_nt(grad_q_lin, w_q) + mm_nt(grad_kv_lin, w_kv)
    back, grad_gain_attn = norm_back(grad_normed_a, hat_attn, inv_attn, gain_a)
    grad_row = (grad_hidden + back).astype(BF)

    blocks = grad_row.reshape(rows, 4, feats)
    me = y * 2 + x

    def block_for(other):
        return lax.dynamic_index_in_dim(blocks, other, 1, False)

    from_x = swap(block_for(me ^ 1), "tx")
    from_y = swap(block_for(me ^ 2), "ty")
    from_both = swap_both(block_for(me ^ 3))
    slot_own = pair(x, block_for(me), from_x, 0)
    slot_other = pair(x, from_y, from_both, 0)
    grad_tokens = jnp.stack(
        [pick(y, slot_other, slot_own), pick(y, slot_own, slot_other)]
    ).astype(F32)

    gain_grads = jnp.stack([grad_gain_attn, grad_gain_mlp])
    gain_high = gain_grads.astype(BF)
    gain_low = (gain_grads - gain_high.astype(F32)).astype(BF)
    gain_rows = jnp.concatenate([gain_high, gain_low, jnp.zeros((12, D), BF)], axis=0)
    wq_blocks = grad_wq.reshape(shards, 2, sub, 4, feats)
    wkv_blocks = grad_wkv.reshape(shards, 2, 4, eighth, feats).transpose(0, 1, 3, 2, 4)
    all_blocks = jnp.concatenate([wq_blocks, wkv_blocks], axis=2)
    all_blocks = all_blocks.transpose(1, 3, 0, 2, 4).reshape(2, 4, shards * (sub + eighth), feats)
    gain_blocks = gain_rows.reshape(16, 4, feats).transpose(1, 0, 2)
    all_blocks = jnp.concatenate(
        [all_blocks, jnp.broadcast_to(gain_blocks, (2,) + gain_blocks.shape)], axis=2
    )
    send_c = lax.dynamic_index_in_dim(all_blocks, 1 - c, 0, False)
    keep_c = lax.dynamic_index_in_dim(all_blocks, c, 0, False)
    chip = (keep_c.astype(F32) + swap(send_c, "ctx").astype(F32)).astype(BF)

    def chip_for(other):
        return lax.dynamic_index_in_dim(chip, other, 0, False)

    plane = (
        chip_for(me).astype(F32)
        + swap(chip_for(me ^ 1), "tx").astype(F32)
        + swap(chip_for(me ^ 2), "ty").astype(F32)
        + swap_both(chip_for(me ^ 3)).astype(F32)
    ).astype(BF)
    gain_part = jnp.broadcast_to(plane[-16:], (shards, 16, feats))
    plane = plane[:-16].reshape(shards, sub + eighth, feats)
    total = along_fsdp(jnp.concatenate([plane, gain_part], axis=1), z)
    grad_query = total[:sub]
    kv_total = total[sub : sub + eighth].astype(BF)
    gain_total = total[sub + eighth :]
    gain_sums = gain_total[:2] + gain_total[2:4]
    kv_pair = pair(x, kv_total, swap(kv_total, "tx"), 0)
    grad_keyval = pair(y, kv_pair, swap(kv_pair, "ty"), 0).astype(F32)

    return (
        outputs,
        grad_tokens,
        grad_query,
        grad_keyval,
        grad_output_proj,
        grad_gateup,
        grad_down,
        gain_sums[0],
        gain_sums[1],
    )


def solution(mesh):
    names = dict(zip(mesh.axis_names, mesh.devices.shape))
    grid = mesh.devices.reshape(names["fsdp"], names["ctx"], 2, names["tp"] // 2)
    split = Mesh(grid, ("fsdp", "ctx", "ty", "tx"))
    tp = ("ty", "tx")
    in_specs = (
        P("fsdp", "ctx", tp),
        P("fsdp"),
        P("fsdp", tp),
        P("fsdp", None),
        P(tp, "fsdp"),
        P(None, "fsdp", tp),
        P(tp, "fsdp"),
        P(tp),
        P(tp),
        P("fsdp", "ctx", tp),
    )
    out_specs = (
        P("fsdp", "ctx", tp),
        P("fsdp", "ctx", tp),
        P(("fsdp", "ctx"), tp),
        P(("fsdp", "ctx"), None),
        P(tp, ("fsdp", "ctx")),
        P(None, ("fsdp", "ctx"), tp),
        P(tp, ("fsdp", "ctx")),
        P(tp),
        P(tp),
    )
    return jax.shard_map(body, mesh=split, in_specs=in_specs, out_specs=out_specs, check_vma=False)
```

```python
import functools
import math

import jax
import jax.numpy as jnp
from jax import lax
from jax.experimental import pallas as pl
from jax.experimental.pallas import tpu as pltpu
from jax.sharding import Mesh
from jax.sharding import PartitionSpec as P

D = 1024
HEAD = 128
WINDOW = 1024
ROWS = 256
SPAN = WINDOW + ROWS
WIDE = 256
EPSILON = 1e-06
NEG = -1e30
LOG2E = math.log2(math.e)
SCALE = HEAD**-0.5
BF = jnp.bfloat16
F32 = jnp.float32
LIMIT = 24 << 20
COST = 1 / 16


def mm(a, b):
    return jnp.dot(a, b, preferred_element_type=F32)


def mm_nt(a, b):
    return lax.dot_general(a, b, (((1,), (1,)), ((), ())), preferred_element_type=F32)


def mm_tn(a, b):
    return lax.dot_general(a, b, (((0,), (0,)), ((), ())), preferred_element_type=F32)


def out(shape, kind):
    return jax.ShapeDtypeStruct(shape, kind)


def cost(flops, nbytes, exps=0):
    flops, nbytes, exps = (int(v * COST) for v in (flops, nbytes, exps))
    return pl.CostEstimate(flops=flops, bytes_accessed=nbytes, transcendentals=exps)


ROW_START, CORE, HALF, ME, SLOT, LENGTHS = 0, 1, 2, 3, 4, 5


def place(info, k):
    return pl.ds(pl.multiple_of((info[ME] ^ k) * WIDE, WIDE), WIDE)


def by_rows(width, rows=ROWS):
    return pl.BlockSpec((rows, width), lambda i, s: (i, 0))


def whole(shape):
    return pl.BlockSpec(shape, lambda i, s: (0,) * len(shape))


def kernel(body, name, grid, args, in_specs, out_specs, outs, work, scratch=(), limit=LIMIT):
    call = pl.pallas_call(
        body,
        grid_spec=pltpu.PrefetchScalarGridSpec(
            num_scalar_prefetch=1,
            grid=(grid,),
            in_specs=[s or whole(a.shape) for s, a in zip(in_specs, args[1:])],
            out_specs=[s or whole(o.shape) for s, o in zip(out_specs, outs)],
            scratch_shapes=scratch,
        ),
        out_shape=outs,
        compiler_params=pltpu.CompilerParams(vmem_limit_bytes=limit),
        cost_estimate=work,
        name=name,
    )
    return call(*args)


def turn(value, cosine, sine):
    return value * cosine + pltpu.roll(value, HEAD // 2, 1) * sine


def prepare_kernel(info, *refs):
    tok_ref, cot_ref, ga_ref, gm_ref, wq_ref, wkv_ref, wo_ref, wgu_ref, wd_ref = refs[:9]
    pieces, cots, qkv_ref, mlp_ref = refs[9:13], refs[13:15], *refs[15:]
    gains = jnp.concatenate(
        [r[...].astype(F32).reshape(1, WIDE) for r in (ga_ref, gm_ref)]
        + [jnp.zeros((14, WIDE), F32)],
        axis=0,
    ).astype(BF)
    rows = tok_ref.shape[1] // 2
    c, x, y = info[CORE], info[HALF], info[SLOT]
    units = wd_ref.shape[0] // 2
    column = pl.ds(pl.multiple_of(c * HEAD, HEAD), HEAD)
    qkv_ref[0] = wq_ref[:, column]
    qkv_ref[1] = wkv_ref[:, column]
    qkv_ref[2] = wo_ref[pl.ds(pl.multiple_of(c * HEAD, HEAD), HEAD), :].T
    for k in range(4):
        half = pl.ds(pl.multiple_of((x ^ (k & 1)) * rows, rows), rows)
        pieces[k][:rows, :] = tok_ref[y ^ (k >> 1), half, :]
        pieces[k][rows:, :] = gains
    for k in range(2):
        half = pl.ds(pl.multiple_of((x ^ k) * rows, rows), rows)
        for slot in range(2):
            time = lax.broadcasted_iota(jnp.int32, (rows, WIDE), 0)
            time = time + info[ROW_START] + ((x ^ k) - x) * rows
            value = cot_ref[y ^ slot, half, :]
            cots[k][slot] = jnp.where(
                time < info[LENGTHS + (y ^ slot)], value.astype(F32), 0.0
            ).astype(BF)
    unit = pl.ds(pl.multiple_of(c * units, HEAD), units)
    mlp_ref[:, :units] = wgu_ref[0, :, unit]
    mlp_ref[:, units : 2 * units] = wgu_ref[1, :, unit]
    mlp_ref[:, 2 * units :] = wd_ref[unit, :].T


def prepare(info, tokens, cotangent, gain_attn, gain_mlp, w_query, w_keyval, w_out, w_gateup, w_down):
    rows = tokens.shape[1] // 2
    depth = w_query.shape[0]
    outs = [out((rows + 16, WIDE), BF)] * 4 + [out((2, rows, WIDE), BF)] * 2
    outs += [
        out((3, depth, HEAD), BF),
        out((depth, 3 * w_down.shape[0] // 2), BF),
    ]
    args = (info, tokens, cotangent, gain_attn, gain_mlp, w_query, w_keyval, w_out, w_gateup, w_down)
    return kernel(
        prepare_kernel, "prepare", 1, args, [None] * 9, [None] * 8, outs, cost(0, 6 << 20), (), 60 << 20
    )


def assemble_kernel(info, *refs):
    for k in range(4):
        for slot in range(2):
            refs[4 + slot][:, place(info, k)] = refs[k][slot ^ (k >> 1)]


def assemble(info, parts):
    rows = parts[0].shape[1]
    return kernel(
        assemble_kernel,
        "assemble",
        1,
        (info, *parts),
        [None] * 4,
        [None] * 2,
        [out((rows, D), BF)] * 2,
        cost(0, 8 << 20),
    )


def project_kernel(info, *refs):
    pieces, (wq_own, wq_core, kv_near, kv_core) = refs[:4], refs[4:8]
    cos_ref, sin_ref, x_ref, gain_ref, normed_ref, q_ref, kv_ref, wkv_ref = refs[8:]
    rows = x_ref.shape[0]
    for k in range(4):
        x_ref[:, place(info, k)] = pieces[k][:rows, :]
        gain_ref[:, place(info, k)] = pieces[k][rows:, :]
    resid = x_ref[...].astype(F32)
    inv = lax.rsqrt(jnp.mean(resid * resid, axis=1, keepdims=True) + EPSILON)
    normed = (resid * inv * gain_ref[0:1, :].astype(F32)).astype(BF)
    normed_ref[...] = normed
    cosine, sine = cos_ref[...], sin_ref[...]
    own_first = info[CORE] == 0
    wkv_ref[:, :HEAD] = jnp.where(own_first, kv_near[1], kv_core[...])
    wkv_ref[:, HEAD:] = jnp.where(own_first, kv_core[...], kv_near[1])
    lin = mm(normed, wkv_ref[...])
    kv_ref[:, :HEAD] = turn(lin[:, :HEAD], cosine, sine).astype(BF)
    kv_ref[:, HEAD:] = lin[:, HEAD:].astype(BF)
    for j in range(4):
        lin = mm(normed, two_heads(wq_own if j < 2 else wq_core, j % 2))
        for i in range(2):
            head = turn(lin[:, i * HEAD : (i + 1) * HEAD], cosine, sine)
            q_ref[:, (2 * j + i) * HEAD : (2 * j + i + 1) * HEAD] = head.astype(BF)


def two_heads(ref, j):
    return jnp.concatenate([ref[2 * j], ref[2 * j + 1]], axis=1)


def project(info, pieces, w_q, w_kv, cosine, sine):
    rows = pieces[0].shape[0] - 16
    return kernel(
        project_kernel,
        "project",
        1,
        (info, *pieces, *w_q, *w_kv, cosine, sine),
        [None] * 10,
        [None] * 6,
        [
            out((rows, D), BF),
            out((16, D), BF),
            out((rows, D), BF),
            out((rows, 8 * HEAD), BF),
            out((rows, 2 * HEAD), BF),
            out((D, 2 * HEAD), BF),
        ],
        cost(2 * rows * D * 10 * HEAD, 8 << 20),
    )


def fill_bias(bias_ref, info, step):
    row = lax.broadcasted_iota(jnp.int32, (ROWS, SPAN), 0)
    col = lax.broadcasted_iota(jnp.int32, (ROWS, SPAN), 1)
    pos = info[ROW_START] - WINDOW + step * ROWS + col
    ahead = col - row - WINDOW
    inside = (ahead <= 0) & (ahead > -WINDOW) & (pos >= 0) & (pos < info[LENGTHS + info[SLOT]])
    bias_ref[...] = jnp.where(inside | (ahead == 0), 0.0, NEG).astype(F32)


def attend_kernel(info, *refs):
    q_ref, far_ref, near_ref, own_ref = refs[:4]
    mixed_ref, lse_ref, kv_ref, bias_ref = refs[4:]
    step = pl.program_id(0)
    rows = own_ref.shape[0]

    @pl.when(step == 0)
    def _():
        kv_ref[:rows, :] = far_ref[...]
        kv_ref[rows : 2 * rows, :] = near_ref[...]
        kv_ref[2 * rows :, :] = own_ref[...]

    fill_bias(bias_ref, info, step)
    here = pl.ds(step * ROWS, SPAN)
    keys = kv_ref[here, :HEAD]
    values = kv_ref[here, HEAD:]
    for h in range(8):
        cols = slice(h * HEAD, (h + 1) * HEAD)
        s = mm_nt(q_ref[:, cols], keys) * (SCALE * LOG2E) + bias_ref[...]
        top = jnp.max(s, axis=1, keepdims=True)
        p = jnp.exp2(s - top)
        total = jnp.sum(p, axis=1, keepdims=True)
        mixed_ref[:, cols] = (mm(p.astype(BF), values) / total).astype(BF)
        lse_ref[:, h : h + 1] = top + jnp.log2(total)


def attend(info, q, far, near, own):
    rows = q.shape[0]
    return kernel(
        attend_kernel,
        "attend",
        rows // ROWS,
        (info, q, far, near, own),
        [by_rows(8 * HEAD)] + [None] * 3,
        [by_rows(8 * HEAD), by_rows(8), None],
        [
            out((rows, 8 * HEAD), BF),
            out((rows, 8), F32),
            out((3 * rows, 2 * HEAD), BF),
        ],
        cost(4 * rows * D * SPAN, 5 << 20, rows * 8 * SPAN),
        [pltpu.VMEM((ROWS, SPAN), F32)],
    )


def project_out_kernel(info, *refs):
    mixed_ref, x_ref, gain_ref, w_o = *refs[:3], refs[3:5]
    hidden_ref, normed_ref = refs[5:]
    hidden = x_ref[...].astype(F32)
    for j in range(4):
        mixed = mixed_ref[:, 2 * j * HEAD : 2 * (j + 1) * HEAD]
        hidden = hidden + mm_nt(mixed, two_heads(w_o[j // 2], j % 2))
    hidden_ref[...] = hidden
    inv = lax.rsqrt(jnp.mean(hidden * hidden, axis=1, keepdims=True) + EPSILON)
    normed_ref[...] = (hidden * inv * gain_ref[1:2, :].astype(F32)).astype(BF)


def project_out(info, mixed, x, gains, w_o):
    rows = x.shape[0]
    return kernel(
        project_out_kernel,
        "project_out",
        rows // ROWS,
        (info, mixed, x, gains, *w_o),
        [by_rows(8 * HEAD), by_rows(D)] + [None] * 3,
        [by_rows(D), by_rows(D)],
        [out((rows, D), F32), out((rows, D), BF)],
        cost(2 * rows * D * D, 7 << 20),
    )


def norm_back_kernel(info, *refs):
    own_ref, cot_ref, hidden_ref, gain_ref, *came_refs = refs[:6]
    gh_ref, ghl_ref, gg_ref = refs[6:]

    @pl.when(pl.program_id(0) == 0)
    def _():
        gg_ref[...] = jnp.zeros_like(gg_ref)

    came = jnp.where(pl.program_id(0) == 0, came_refs[0][...], came_refs[1][...])
    grad = own_ref[...].astype(F32) + came.astype(F32)
    hidden = hidden_ref[...]
    inv = lax.rsqrt(jnp.mean(hidden * hidden, axis=1, keepdims=True) + EPSILON)
    hat = hidden * inv
    gg_ref[0:1, :] += jnp.sum(grad * hat, axis=0, keepdims=True)
    g = grad * gain_ref[1:2, :].astype(F32)
    dots = jnp.mean(g * hat, axis=1, keepdims=True)
    grad_hidden = cot_ref[...].astype(F32) + inv * (g - hat * dots)
    gh_ref[...] = grad_hidden
    ghl_ref[...] = grad_hidden.astype(BF)


def norm_back(info, own, came, cot, hidden, gains):
    rows = hidden.shape[0]
    return kernel(
        norm_back_kernel,
        "norm_back",
        rows // ROWS,
        (info, own, cot, hidden, gains, *came),
        [by_rows(D)] * 3 + [None] * 3,
        [by_rows(D), by_rows(D), None],
        [out((rows, D), F32), out((rows, D), BF), out((8, D), F32)],
        cost(20 * rows * D, 10 << 20),
    )


def attend_back_kernel(info, *refs):
    low_ref, cos_ref, sin_ref, q_ref, kv_ref, mixed_ref, lse_ref = refs[:7]
    w_o = refs[7:9]
    gq_ref, far_ref, near_ref, here_ref, gkv_ref, bias_ref = refs[9:]
    step = pl.program_id(0)
    rows = here_ref.shape[0]

    @pl.when(step == 0)
    def _():
        gkv_ref[...] = jnp.zeros_like(gkv_ref)

    low = low_ref[...]
    fill_bias(bias_ref, info, step)
    here = pl.ds(step * ROWS, SPAN)
    keys = kv_ref[here, :HEAD]
    values = kv_ref[here, HEAD:]
    for j in range(4):
        two = mm(low, two_heads(w_o[j // 2], j % 2))
        for i in range(2):
            h = 2 * j + i
            cols = slice(h * HEAD, (h + 1) * HEAD)
            q = q_ref[:, cols]
            gm = two[:, i * HEAD : (i + 1) * HEAD].astype(BF)
            s = mm_nt(q, keys) * (SCALE * LOG2E) + bias_ref[...]
            p = jnp.exp2(s - lse_ref[:, h : h + 1])
            gp = mm_nt(gm, values)
            inner = jnp.sum(
                gm.astype(F32) * mixed_ref[:, cols].astype(F32), axis=1, keepdims=True
            )
            gs = (p * (gp - inner)).astype(BF)
            gq = mm(gs, keys) * SCALE
            gq_ref[:, cols] = turn(gq, cos_ref[...], -sin_ref[...]).astype(BF)
            gkv_ref[here, :HEAD] += mm_tn(gs, q) * SCALE
            gkv_ref[here, HEAD:] += mm_tn(p.astype(BF), gm)

    @pl.when(step == pl.num_programs(0) - 1)
    def _():
        far_ref[...] = gkv_ref[:rows, :].astype(BF)
        near_ref[...] = gkv_ref[rows : 2 * rows, :].astype(BF)
        here_ref[...] = gkv_ref[2 * rows :, :]


def attend_back(info, low, cosine, sine, q, kv, mixed, lse, w_o):
    rows = q.shape[0]
    wide = by_rows(8 * HEAD)
    return kernel(
        attend_back_kernel,
        "attend_back",
        rows // ROWS,
        (info, low, cosine, sine, q, kv, mixed, lse, *w_o),
        [by_rows(D), by_rows(HEAD), by_rows(HEAD), wide, None, wide, by_rows(8), None, None],
        [wide] + [None] * 3,
        [out((rows, 8 * HEAD), BF)] + [out((rows, 2 * HEAD), k) for k in (BF, BF, F32)],
        cost(10 * rows * D * (SPAN + HEAD), 12 << 20, rows * 8 * SPAN),
        [pltpu.VMEM(kv.shape, F32), pltpu.VMEM((ROWS, SPAN), F32)],
        60 << 20,
    )


def project_back_kernel(info, *refs):
    gq_ref, here_ref, near_ref, far_ref, cos_ref, sin_ref, x_ref, gain_ref, gh_ref = refs[:9]
    wq_own, wq_core, wkv_ref = refs[9:12]
    gkv_ref, gg_ref, *piece_refs = refs[12:18]
    buffer_ref = refs[18]

    @pl.when(pl.program_id(0) == 0)
    def _():
        gg_ref[...] = jnp.zeros_like(gg_ref)

    grad = here_ref[...] + near_ref[...].astype(F32) + far_ref[...].astype(F32)
    gkv_ref[:, :HEAD] = turn(grad[:, :HEAD], cos_ref[...], -sin_ref[...]).astype(BF)
    gkv_ref[:, HEAD:] = grad[:, HEAD:].astype(BF)
    normed_grad = mm_nt(gkv_ref[...], wkv_ref[...])
    for j in range(4):
        weights = two_heads(wq_own if j < 2 else wq_core, j % 2)
        normed_grad = normed_grad + mm_nt(gq_ref[:, 2 * j * HEAD : 2 * (j + 1) * HEAD], weights)
    resid = x_ref[...].astype(F32)
    inv = lax.rsqrt(jnp.mean(resid * resid, axis=1, keepdims=True) + EPSILON)
    hat = resid * inv
    gg_ref[0:1, :] += jnp.sum(normed_grad * hat, axis=0, keepdims=True)
    g = normed_grad * gain_ref[0:1, :].astype(F32)
    dots = jnp.mean(g * hat, axis=1, keepdims=True)
    buffer_ref[...] = gh_ref[...] + inv * (g - hat * dots)
    for k in range(4):
        piece_refs[k][...] = buffer_ref[:, place(info, k)].astype(BF)


def project_back(info, gq, grad_kv, near, far, cosine, sine, x, gains, grad_hidden, w_q, w_kv):
    rows = gq.shape[0]
    steps = rows // ROWS
    pair_rows = by_rows(2 * HEAD)
    return kernel(
        project_back_kernel,
        "project_back",
        steps,
        (info, gq, grad_kv, near, far, cosine, sine, x, gains, grad_hidden, *w_q, w_kv),
        [
            by_rows(8 * HEAD),
            pair_rows,
            pair_rows,
            pair_rows,
            by_rows(HEAD),
            by_rows(HEAD),
            by_rows(D),
            None,
            by_rows(D),
            None,
            None,
            None,
        ],
        [pair_rows, None] + [by_rows(WIDE)] * 4,
        [out((rows, 2 * HEAD), BF), out((8, D), F32)] + [out((rows, WIDE), BF)] * 4,
        cost(2 * rows * D * 10 * HEAD, 10 << 20),
        [pltpu.VMEM((ROWS, D), F32)],
    )


def halves(ref, info, shards, core):
    sub = D // shards // 2
    at_core = info[CORE] ^ core
    return jnp.concatenate(
        [
            ref[:, pl.ds(pl.multiple_of(d * 2 * sub + at_core * sub, HEAD), sub)]
            for d in range(shards)
        ],
        axis=1,
    )


def head_grads_kernel(shards, info, *refs):
    sub = D // shards // 2
    for at_pair in range(2):
        left_ref, right_ref = refs[2 * at_pair : 2 * at_pair + 2]
        for core in range(2):
            mine = halves(left_ref, info, shards, core)
            for j in range(2):
                cols = []
                for k in (2 * j, 2 * j + 1):
                    for kc in (core, 1 - core):
                        cols.append(right_ref[:, (kc * 4 + k) * HEAD : (kc * 4 + k + 1) * HEAD])
                grad = mm_tn(mine, jnp.concatenate(cols, axis=1)).astype(BF)
                for i in range(2):
                    part = grad[:, i * WIDE : (i + 1) * WIDE].reshape(shards, sub, WIDE)
                    refs[4 + core][2 * j + i, :, at_pair * sub : (at_pair + 1) * sub, :] = part


def key_grads_kernel(shards, info, *refs):
    normed_ref, gkv_ref, ga_ref, gm_ref = refs[:4]
    sub = D // shards // 2
    gains = [r[0:1, k * WIDE : (k + 1) * WIDE] for r in (ga_ref, gm_ref) for k in range(4)]
    gains = jnp.concatenate(gains + [jnp.zeros((8, WIDE), F32)], axis=0).astype(BF)
    for core in range(2):
        grad = mm_tn(halves(normed_ref, info, shards, core), gkv_ref[...]).astype(BF)
        for d in range(shards):
            refs[4 + core][d, :sub, :] = grad[d * sub : (d + 1) * sub, :]
            refs[4 + core][d, sub:, :] = gains


def key_grads(info, c, shards, normed, gkv, ga, gm):
    sub = D // shards // 2
    if sub % HEAD:
        keys = mm_tn(normed, gkv).astype(BF).reshape(shards, 2, sub, WIDE)
        gains = jnp.concatenate([ga[0].reshape(4, WIDE), gm[0].reshape(4, WIDE)])
        gains = jnp.concatenate([gains, jnp.zeros((8, WIDE), F32)]).astype(BF)
        gains = jnp.broadcast_to(gains, (shards, 16, WIDE))
        return [jnp.concatenate([at(keys, c ^ core, 1), gains], axis=1) for core in range(2)]
    return kernel(
        functools.partial(key_grads_kernel, shards),
        "key_grads",
        1,
        (info, normed, gkv, ga, gm),
        [None] * 4,
        [None] * 2,
        [out((shards, sub + 16, WIDE), BF)] * 2,
        cost(2 * normed.shape[0] * D * WIDE, 2 << 20),
    )


def head_grads(info, c, shards, pairs):
    rows = pairs[0].shape[0]
    sub = D // shards // 2
    if sub % HEAD:
        parts = [[], []]
        for left, right in (pairs[:2], pairs[2:]):
            grad = mm_tn(left, right).astype(BF).reshape(shards, 2, sub, 2, 4, HEAD)
            for core in range(2):
                mine = at(grad, c ^ core, 1)
                mine = mine[:, :, ::-1] if core else mine
                mine = mine.transpose(3, 0, 1, 2, 4).reshape(4, shards, sub, WIDE)
                parts[core].append(mine)
        return [jnp.concatenate(p, axis=2) for p in parts]
    return kernel(
        functools.partial(head_grads_kernel, shards),
        "head_grads",
        1,
        (info, *pairs),
        [None] * 4,
        [None] * 2,
        [out((4, shards, 2 * sub, WIDE), BF)] * 2,
        cost(4 * rows * D * D, 10 << 20),
    )


def sum_parts_kernel(info, *refs):
    for k in range(4):
        refs[2 + k][...] = (refs[0][k].astype(F32) + refs[1][k].astype(F32)).astype(BF)


def sum_parts(info, mine, other):
    return kernel(
        sum_parts_kernel,
        "sum_parts",
        1,
        (info, mine, other),
        [None] * 2,
        [None] * 4,
        [out(mine.shape[1:], BF)] * 4,
        cost(0, 6 << 20),
    )


def mlp_kernel(units, first, cut_up, info, *refs):
    rows, cot = refs[0][...], refs[1][...]
    weights = refs[2:4]
    active_ref, ggu_ref, branch_ref, *gn_refs = refs[4 if first else 6 :]
    root = math.sqrt(2 / math.pi)
    grad_normed = 0.0 if first else refs[4][...].astype(F32)
    branch = 0.0 if first else refs[5][...].astype(F32)
    for part in range(2):
        w_gu = weights[part][:, : 2 * units]
        w_dt = weights[part][:, 2 * units :]
        lin = mm(rows, w_gu)
        gate, up = lin[:, :units], lin[:, units:]
        grad_active = mm(cot, w_dt)
        square = gate * gate
        tanh = jnp.tanh(root * gate * (1.0 + 0.044715 * square))
        side = 0.5 * (1.0 + tanh)
        gelu = gate * side
        slope = side + gelu * (1.0 - tanh) * (root + 3 * 0.044715 * root * square)
        active = (gelu * up).astype(BF)
        grad_gu = jnp.concatenate(
            [(grad_active * up * slope).astype(BF), (grad_active * gelu).astype(BF)], axis=1
        )
        active_ref[:, part * units : (part + 1) * units] = active
        ggu_ref[:, part * 2 * units : (part + 1) * 2 * units] = grad_gu
        grad_normed = grad_normed + mm_nt(grad_gu, w_gu)
        branch = branch + mm_nt(active, w_dt)
    branch_ref[...] = branch.astype(BF)
    if not cut_up:
        gn_refs[0][...] = grad_normed.astype(BF)
    else:
        for i in range(2):

            @pl.when(pl.program_id(0) == i)
            def _():
                gn_refs[i][...] = grad_normed.astype(BF)


def mlp(info, rows, cot, weights, before=(), cut_up=False):
    count = rows.shape[0]
    units = weights[0].shape[1] // 3
    widths = (2 * units, 4 * units, D)
    outs = [out((count, w), BF) for w in widths]
    outs += [out((ROWS, D), BF)] * 2 if cut_up else [out((count, D), BF)]
    return kernel(
        functools.partial(mlp_kernel, units, not before, cut_up),
        "mlp",
        count // ROWS,
        (info, rows, cot, *weights, *before),
        [by_rows(D)] * 2 + [None] * 2 + [by_rows(D)] * len(before),
        [by_rows(w) for w in widths] + ([None] * 2 if cut_up else [by_rows(D)]),
        outs,
        cost(24 * count * D * units, 14 << 20, count * 2 * units),
    )


def unit_grads_kernel(info, *refs):
    rows_refs, cot_refs, gu_refs, act_refs, out_refs = (refs[i : i + 2] for i in range(0, 10, 2))
    units = act_refs[0].shape[1] // 2
    for part in range(2):
        gu = slice(part * 2 * units, (part + 1) * 2 * units)
        act = slice(part * units, (part + 1) * units)
        up = mm_tn(rows_refs[0][...], gu_refs[0][:, gu]) + mm_tn(rows_refs[1][...], gu_refs[1][:, gu])
        down = mm_tn(cot_refs[0][...], act_refs[0][:, act]) + mm_tn(cot_refs[1][...], act_refs[1][:, act])
        out_refs[part][:, : 2 * units] = up.astype(BF)
        out_refs[part][:, 2 * units :] = down.astype(BF)


def unit_grads(info, rows, cots, grads, actives):
    count = rows[0].shape[0]
    units = actives[0].shape[1] // 2
    columns = pl.BlockSpec((count, WIDE), lambda i, s: (0, i))
    return kernel(
        unit_grads_kernel,
        "unit_grads",
        D // WIDE,
        (info, *rows, *cots, *grads, *actives),
        [columns] * 4 + [None] * 4,
        [pl.BlockSpec((WIDE, 3 * units), lambda i, s: (i, 0))] * 2,
        [out((D, 3 * units), BF)] * 2,
        cost(24 * count * D * units, 14 << 20),
    )


def split_kernel(info, *refs):
    own_ref, hidden_ref, far_ref = refs[:3]
    pieces, buffer_ref = refs[3:7], refs[7]
    for slot in range(2):
        total = own_ref[...].astype(F32) + hidden_ref[...] if slot == 0 else far_ref[...].astype(F32)
        buffer_ref[...] = total
        for k in range(4):
            pieces[k][slot ^ (k >> 1)] = buffer_ref[:, place(info, k)].astype(BF)


def split(info, own, hidden, far):
    rows = own.shape[0]
    return kernel(
        split_kernel,
        "split",
        1,
        (info, own, hidden, far),
        [None] * 3,
        [None] * 4,
        [out((2, rows, WIDE), BF)] * 4,
        cost(0, 8 << 20),
        [pltpu.VMEM((rows, D), F32)],
    )


def swap(value, axis):
    return lax.ppermute(value, axis, [(0, 1), (1, 0)])


def swap_both(value):
    return lax.ppermute(value, ("ty", "tx"), [(i, i ^ 3) for i in range(4)])


def to_next(value, back=False):
    pairs = [(0, 1), (1, 2), (2, 3), (3, 0)]
    return lax.ppermute(value, ("ctx", "tx"), [p[::-1] for p in pairs] if back else pairs)


def exchange(parts):
    return [parts[0], swap(parts[1], "tx"), swap(parts[2], "ty"), swap_both(parts[3])]


def after(value, *others):
    return lax.optimization_barrier((value, others))[0]


def pick(flag, ones, zeros):
    return jnp.where(flag == 1, ones, zeros)


def pair(flag, own, other, axis):
    return jnp.concatenate([pick(flag, other, own), pick(flag, own, other)], axis=axis)


def half_at(value, index, axis):
    size = value.shape[axis] // 2
    return lax.dynamic_slice_in_dim(value, index * size, size, axis)


def at(value, index, axis=0):
    return lax.dynamic_index_in_dim(value, index, axis, False)


def add(*values):
    return sum(v.astype(F32) for v in values)


DIRECT = 4


def to_shard(value, step):
    shards = lax.axis_size("fsdp")
    return lax.ppermute(value, "fsdp", [(i, (i + step) % shards) for i in range(shards)])


def fsdp_gather(part, axis):
    shards = lax.axis_size("fsdp")
    if shards > DIRECT:
        return lax.all_gather(part, "fsdp", axis=axis, tiled=True)
    size = part.shape[axis]
    z = lax.axis_index("fsdp")
    shape = part.shape[:axis] + (shards * size,) + part.shape[axis + 1 :]
    full = lax.dynamic_update_slice_in_dim(jnp.zeros(shape, part.dtype), part, z * size, axis)
    for step in range(1, shards):
        origin = (z - step) % shards
        full = lax.dynamic_update_slice_in_dim(full, to_shard(part, step), origin * size, axis)
    return full


def fsdp_scatter(parts):
    shards = lax.axis_size("fsdp")
    if shards > DIRECT:
        return lax.psum_scatter(parts, "fsdp", scatter_dimension=0, tiled=False).astype(F32)
    z = lax.axis_index("fsdp")
    came = [to_shard(at(parts, (z + step) % shards), step) for step in range(1, shards)]
    return add(at(parts, z), *came)


def fsdp_halve(parts):
    shards = lax.axis_size("fsdp")
    if shards > DIRECT:
        return lax.psum_scatter(parts, "fsdp", scatter_dimension=0, tiled=False)
    z = lax.axis_index("fsdp")
    count = shards // 2
    while count:
        parts = parts.reshape((2, count) + parts.shape[1:])
        side = (z // count) % 2
        came = lax.ppermute(at(parts, 1 - side), "fsdp", [(i, i ^ count) for i in range(shards)])
        parts = add(at(parts, side), came).astype(BF)
        count //= 2
    return parts[0]


def body(
    tokens, lengths, w_query, w_keyval, w_out, w_gateup, w_down, gain_attn, gain_mlp, cotangent
):
    shards = lax.axis_size("fsdp")
    z, c = lax.axis_index("fsdp"), lax.axis_index("ctx")
    y, x = lax.axis_index("ty"), lax.axis_index("tx")
    me = 2 * y + x
    seq_rows = tokens.shape[1]
    rows = seq_rows // 2
    depth = w_query.shape[0]
    sub = depth // 2
    units = w_gateup.shape[2] // 2
    row_start = c * seq_rows + x * rows
    info = jnp.stack(
        [row_start, c, x, me, y, lengths[0], lengths[1]]
    ).astype(jnp.int32)

    *sends, qkv_part, mlp_part = prepare(
        info, tokens, cotangent, gain_attn, gain_mlp, w_query, w_keyval, w_out, w_gateup, w_down
    )

    qkv = fsdp_gather(qkv_part, 1)
    pieces = exchange(sends[:4])
    own_cot, x_cot = sends[4:]
    qkv, mlp_part = after([qkv, mlp_part], pieces)
    w_near = lax.all_gather(mlp_part, "fsdp", axis=0, tiled=True)
    w_q = jnp.stack(exchange([qkv[0]] * 4))
    w_q = [w_q, swap(w_q, "ctx")]
    w_kv = [qkv, swap(qkv[1], "ctx")]
    qkv_late, own_cot, x_cot = after([qkv, own_cot, x_cot], w_q[0])
    cot_x, cot_y = swap(x_cot, "tx"), swap(own_cot, "ty")

    half_width = HEAD // 2
    freq = 10000.0 ** (-jnp.arange(half_width, dtype=F32) / half_width)
    angles = (row_start + jnp.arange(rows, dtype=jnp.int32)).astype(F32)[:, None] * freq[None, :]
    cosine, sine = jnp.cos(angles), jnp.sin(angles)
    cosine = jnp.concatenate([cosine, cosine], axis=1)
    sine = jnp.concatenate([-sine, sine], axis=1)

    x_rows, gain_rows, normed_attn, q, kv_own, w_kv = project(
        info, pieces, w_q, w_kv, cosine, sine
    )
    kv_near, kv_far = to_next(kv_own), swap(kv_own, "ctx")
    w_o = exchange([after(qkv_late[2], kv_own)] * 4)
    q, cot_x, cot_y = after([q, cot_x, cot_y], kv_near)
    cot_both = swap(cot_x, "ty")
    mixed, lse, kv = attend(info, q, kv_far, kv_near, kv_own)
    w_o, w_near, cot_both, mixed = after([w_o, w_near, cot_both, mixed])
    w_o = jnp.stack(w_o)
    w_o = [w_o, swap(w_o, "ctx")]
    w_far = swap(w_near, "tx")
    w_near = [w_near, swap(w_near, "ctx")]
    hidden, normed_mlp = project_out(info, mixed, x_rows, gain_rows, w_o)
    cot_parts = after([own_cot, cot_x, cot_y, cot_both], normed_mlp)
    cots = assemble(info, cot_parts)

    far = swap(normed_mlp, "ty")
    near_act, near_gu, *near_sums = mlp(info, normed_mlp, cots[0], w_near)
    far = after(far, near_act)
    far_act, far_gu, *far_sums = mlp(info, far, cots[1], w_near)
    mlp_rows = [normed_mlp, far]

    def over_cores(grads):
        return add(grads[0], swap(grads[1], "ctx")).astype(BF)

    def over_fsdp(grads):
        return lax.psum_scatter(grads, "fsdp", scatter_dimension=0, tiled=True)

    own_grads = unit_grads(info, mlp_rows, cots, [near_gu, far_gu], [near_act, far_act])
    w_far, own_grads = after([w_far, own_grads])
    w_far = [w_far, swap(w_far, "ctx")]
    own_grads, w_far = after([over_cores(own_grads), w_far])
    own_sums = over_fsdp(own_grads)
    far_act, far_gu, far_branch, *gn_y = mlp(
        info, far, cots[1], w_far, [far_sums[1], far_sums[0]], True
    )
    near_sums = after(near_sums, gn_y)
    gn_y = [swap(g, "ty") for g in gn_y]
    near_act, near_gu, branch, gn = mlp(
        info, normed_mlp, cots[0], w_far, [near_sums[1], near_sums[0]]
    )
    out_parts = split(info, branch, hidden, after(far_branch, gn))
    gn_y[0], near_act = after([gn_y[0], near_act], out_parts)
    other_grads = unit_grads(info, mlp_rows, cots, [near_gu, far_gu], [near_act, far_act])
    gn_y = after(gn_y, other_grads)

    grad_hidden, grad_low, gg_mlp = norm_back(
        info, gn, gn_y, cots[0], hidden, gain_rows
    )

    other_grads, grad_low = after([over_cores(after(other_grads, gn_y)), grad_low])
    other_sums = over_fsdp(other_grads)
    out_came = exchange(after(out_parts, gn_y))
    grad_q, kv_far, kv_near, kv_here = attend_back(
        info, grad_low, cosine, sine, q, kv, mixed, lse, w_o
    )
    kv_near, kv_far = to_next(kv_near, True), swap(kv_far, "ctx")
    grad_q, out_came, own_sums = after([grad_q, out_came, own_sums])
    mine, other = head_grads(
        info, c, shards, after([normed_attn, grad_q, grad_low, mixed], kv_near)
    )
    chip = sum_parts(info, mine, swap(other, "ctx"))
    plane = exchange(chip)
    kv_here = after(kv_here, chip)
    grad_kv, gg_attn, *grad_pieces = project_back(
        info,
        grad_q,
        kv_here,
        kv_near,
        kv_far,
        cosine,
        sine,
        x_rows,
        gain_rows,
        grad_hidden,
        w_q,
        w_kv,
    )
    mine, other = key_grads(info, c, shards, normed_attn, grad_kv, gg_attn, gg_mlp)
    keys = add(mine, swap(other, "ctx")).astype(BF)
    keys, other_sums, grad_pieces, plane = after([keys, other_sums, grad_pieces, plane])
    grad_came = exchange(grad_pieces)
    plane = add(*plane).astype(BF)
    keys, other_sums, grad_came[1], grad_came[2] = after(
        [keys, other_sums, grad_came[1], grad_came[2]], plane
    )
    total = fsdp_scatter(plane)
    from_x = swap(other_sums, "tx")
    keys = fsdp_halve(keys)
    keys = add(keys, swap(keys, "tx")).astype(BF)
    keys = add(keys, swap(keys, "ty"))
    total = [pair(c, g[:, :HEAD], g[:, HEAD:], 1) for g in (total[:sub], total[sub:])]
    grad_query, grad_output_proj = total[0], total[1].T
    grad_keyval = keys[:sub]
    gain_sums = [at(keys[sub + 4 * i : sub + 4 * i + 4], me) for i in range(2)]

    came = grad_came
    slot_own = pair(x, came[0], came[1], 0)
    slot_other = pair(x, came[2], came[3], 0)
    grad_tokens = jnp.stack(
        [pick(y, slot_other, slot_own), pick(y, slot_own, slot_other)]
    ).astype(F32)

    halves_out = [add(out_came[0], out_came[2]), add(out_came[1], out_came[3])]
    outputs = pair(x, *(h.astype(BF) for h in halves_out), 1)
    outputs = jnp.stack([pick(y, outputs[1], outputs[0]), pick(y, outputs[0], outputs[1])])

    mlp_grads = add(own_sums, from_x).astype(BF)
    mlp_other = swap(half_at(mlp_grads, 1 - c, 0), "ctx")
    mlp_own = half_at(mlp_grads, c, 0)

    def units_of(i):
        span = slice(i * units, (i + 1) * units)
        return pair(c, mlp_own[:, span], mlp_other[:, span], 1).astype(F32)

    grad_gateup = jnp.stack([units_of(0), units_of(1)])
    grad_down = units_of(2).T

    return (
        outputs,
        grad_tokens,
        grad_query,
        grad_keyval,
        grad_output_proj,
        grad_gateup,
        grad_down,
        gain_sums[0],
        gain_sums[1],
    )


def solution(mesh):
    names = dict(zip(mesh.axis_names, mesh.devices.shape))
    grid = mesh.devices.reshape(names["fsdp"], names["ctx"], 2, names["tp"] // 2)
    split = Mesh(grid, ("fsdp", "ctx", "ty", "tx"))
    tp = ("ty", "tx")
    in_specs = (
        P("fsdp", "ctx", tp),
        P("fsdp"),
        P("fsdp", tp),
        P("fsdp", None),
        P(tp, "fsdp"),
        P(None, "fsdp", tp),
        P(tp, "fsdp"),
        P(tp),
        P(tp),
        P("fsdp", "ctx", tp),
    )
    out_specs = (
        P("fsdp", "ctx", tp),
        P("fsdp", "ctx", tp),
        P(("fsdp", "ctx"), tp),
        P(("fsdp", "ctx"), None),
        P(tp, ("fsdp", "ctx")),
        P(None, ("fsdp", "ctx"), tp),
        P(tp, ("fsdp", "ctx")),
        P(tp),
        P(tp),
    )
    return jax.shard_map(body, mesh=split, in_specs=in_specs, out_specs=out_specs, check_vma=False)
```

```python
import functools
import math

import jax
import jax.numpy as jnp
from jax import lax
from jax.experimental import pallas as pl
from jax.experimental.pallas import tpu as pltpu
from jax.sharding import Mesh
from jax.sharding import PartitionSpec as P

D = 1024
HEAD = 128
WINDOW = 1024
ROWS = 256
SPAN = WINDOW + ROWS
WIDE = 256
EPSILON = 1e-06
NEG = -1e30
LOG2E = math.log2(math.e)
SCALE = HEAD**-0.5
BF = jnp.bfloat16
F32 = jnp.float32
LIMIT = 24 << 20
COST = 1 / 16


def mm(a, b):
    return jnp.dot(a, b, preferred_element_type=F32)


def mm_nt(a, b):
    return lax.dot_general(a, b, (((1,), (1,)), ((), ())), preferred_element_type=F32)


def mm_tn(a, b):
    return lax.dot_general(a, b, (((0,), (0,)), ((), ())), preferred_element_type=F32)


def out(shape, kind):
    return jax.ShapeDtypeStruct(shape, kind)


def cost(flops, nbytes, exps=0):
    flops, nbytes, exps = (int(v * COST) for v in (flops, nbytes, exps))
    return pl.CostEstimate(flops=flops, bytes_accessed=nbytes, transcendentals=exps)


ROW_START, CORE, HALF, ME, SLOT, LENGTHS = 0, 1, 2, 3, 4, 5


def place(info, k):
    return pl.ds(pl.multiple_of((info[ME] ^ k) * WIDE, WIDE), WIDE)


def by_rows(width, rows=ROWS):
    return pl.BlockSpec((rows, width), lambda i, s: (i, 0))


def whole(shape):
    return pl.BlockSpec(shape, lambda i, s: (0,) * len(shape))


def kernel(body, name, grid, args, in_specs, out_specs, outs, work, scratch=(), limit=LIMIT):
    call = pl.pallas_call(
        body,
        grid_spec=pltpu.PrefetchScalarGridSpec(
            num_scalar_prefetch=1,
            grid=(grid,),
            in_specs=[s or whole(a.shape) for s, a in zip(in_specs, args[1:])],
            out_specs=[s or whole(o.shape) for s, o in zip(out_specs, outs)],
            scratch_shapes=scratch,
        ),
        out_shape=outs,
        compiler_params=pltpu.CompilerParams(vmem_limit_bytes=limit),
        cost_estimate=work,
        name=name,
    )
    return call(*args)


def turn(value, cosine, sine):
    return value * cosine + pltpu.roll(value, HEAD // 2, 1) * sine


def prepare_kernel(info, *refs):
    tok_ref, cot_ref, ga_ref, gm_ref, wq_ref, wkv_ref, wo_ref, wgu_ref, wd_ref = refs[:9]
    pieces, cots, qkv_ref, mlp_ref = refs[9:13], refs[13:15], *refs[15:]
    gains = jnp.concatenate(
        [r[...].astype(F32).reshape(1, WIDE) for r in (ga_ref, gm_ref)]
        + [jnp.zeros((14, WIDE), F32)],
        axis=0,
    ).astype(BF)
    rows = tok_ref.shape[1] // 2
    c, x, y = info[CORE], info[HALF], info[SLOT]
    units = wd_ref.shape[0] // 2
    column = pl.ds(pl.multiple_of(c * HEAD, HEAD), HEAD)
    qkv_ref[0] = wq_ref[:, column]
    qkv_ref[1] = wkv_ref[:, column]
    qkv_ref[2] = wo_ref[pl.ds(pl.multiple_of(c * HEAD, HEAD), HEAD), :].T
    for k in range(4):
        half = pl.ds(pl.multiple_of((x ^ (k & 1)) * rows, rows), rows)
        pieces[k][:rows, :] = tok_ref[y ^ (k >> 1), half, :]
        pieces[k][rows:, :] = gains
    for k in range(2):
        half = pl.ds(pl.multiple_of((x ^ k) * rows, rows), rows)
        for slot in range(2):
            time = lax.broadcasted_iota(jnp.int32, (rows, WIDE), 0)
            time = time + info[ROW_START] + ((x ^ k) - x) * rows
            value = cot_ref[y ^ slot, half, :]
            cots[k][slot] = jnp.where(
                time < info[LENGTHS + (y ^ slot)], value.astype(F32), 0.0
            ).astype(BF)
    unit = pl.ds(pl.multiple_of(c * units, HEAD), units)
    mlp_ref[:, :units] = wgu_ref[0, :, unit]
    mlp_ref[:, units : 2 * units] = wgu_ref[1, :, unit]
    mlp_ref[:, 2 * units :] = wd_ref[unit, :].T


def prepare(info, tokens, cotangent, gain_attn, gain_mlp, w_query, w_keyval, w_out, w_gateup, w_down):
    rows = tokens.shape[1] // 2
    depth = w_query.shape[0]
    outs = [out((rows + 16, WIDE), BF)] * 4 + [out((2, rows, WIDE), BF)] * 2
    outs += [
        out((3, depth, HEAD), BF),
        out((depth, 3 * w_down.shape[0] // 2), BF),
    ]
    args = (info, tokens, cotangent, gain_attn, gain_mlp, w_query, w_keyval, w_out, w_gateup, w_down)
    return kernel(
        prepare_kernel, "prepare", 1, args, [None] * 9, [None] * 8, outs, cost(0, 6 << 20), (), 60 << 20
    )


def assemble_kernel(info, *refs):
    for k in range(4):
        for slot in range(2):
            refs[4 + slot][:, place(info, k)] = refs[k][slot ^ (k >> 1)]


def assemble(info, parts):
    rows = parts[0].shape[1]
    return kernel(
        assemble_kernel,
        "assemble",
        1,
        (info, *parts),
        [None] * 4,
        [None] * 2,
        [out((rows, D), BF)] * 2,
        cost(0, 8 << 20),
    )


def project_kernel(info, *refs):
    pieces, (wq_own, wq_core, kv_near, kv_core) = refs[:4], refs[4:8]
    cos_ref, sin_ref, x_ref, gain_ref, normed_ref, q_ref, kv_ref, wkv_ref = refs[8:]
    rows = x_ref.shape[0]
    for k in range(4):
        x_ref[:, place(info, k)] = pieces[k][:rows, :]
        gain_ref[:, place(info, k)] = pieces[k][rows:, :]
    resid = x_ref[...].astype(F32)
    inv = lax.rsqrt(jnp.mean(resid * resid, axis=1, keepdims=True) + EPSILON)
    normed = (resid * inv * gain_ref[0:1, :].astype(F32)).astype(BF)
    normed_ref[...] = normed
    cosine, sine = cos_ref[...], sin_ref[...]
    own_first = info[CORE] == 0
    wkv_ref[:, :HEAD] = jnp.where(own_first, kv_near[1], kv_core[...])
    wkv_ref[:, HEAD:] = jnp.where(own_first, kv_core[...], kv_near[1])
    lin = mm(normed, wkv_ref[...])
    kv_ref[:, :HEAD] = turn(lin[:, :HEAD], cosine, sine).astype(BF)
    kv_ref[:, HEAD:] = lin[:, HEAD:].astype(BF)
    for j in range(4):
        lin = mm(normed, two_heads(wq_own if j < 2 else wq_core, j % 2))
        for i in range(2):
            head = turn(lin[:, i * HEAD : (i + 1) * HEAD], cosine, sine)
            q_ref[:, (2 * j + i) * HEAD : (2 * j + i + 1) * HEAD] = head.astype(BF)


def two_heads(ref, j):
    return jnp.concatenate([ref[2 * j], ref[2 * j + 1]], axis=1)


def project(info, pieces, w_q, w_kv, cosine, sine):
    rows = pieces[0].shape[0] - 16
    return kernel(
        project_kernel,
        "project",
        1,
        (info, *pieces, *w_q, *w_kv, cosine, sine),
        [None] * 10,
        [None] * 6,
        [
            out((rows, D), BF),
            out((16, D), BF),
            out((rows, D), BF),
            out((rows, 8 * HEAD), BF),
            out((rows, 2 * HEAD), BF),
            out((D, 2 * HEAD), BF),
        ],
        cost(2 * rows * D * 10 * HEAD, 8 << 20),
    )


def fill_bias(bias_ref, info, step):
    row = lax.broadcasted_iota(jnp.int32, (ROWS, SPAN), 0)
    col = lax.broadcasted_iota(jnp.int32, (ROWS, SPAN), 1)
    pos = info[ROW_START] - WINDOW + step * ROWS + col
    ahead = col - row - WINDOW
    inside = (ahead <= 0) & (ahead > -WINDOW) & (pos >= 0) & (pos < info[LENGTHS + info[SLOT]])
    bias_ref[...] = jnp.where(inside | (ahead == 0), 0.0, NEG).astype(F32)


def attend_kernel(info, *refs):
    q_ref, far_ref, near_ref, own_ref = refs[:4]
    mixed_ref, lse_ref, kv_ref, bias_ref = refs[4:]
    step = pl.program_id(0)
    rows = own_ref.shape[0]

    @pl.when(step == 0)
    def _():
        kv_ref[:rows, :] = far_ref[...]
        kv_ref[rows : 2 * rows, :] = near_ref[...]
        kv_ref[2 * rows :, :] = own_ref[...]

    fill_bias(bias_ref, info, step)
    here = pl.ds(step * ROWS, SPAN)
    keys = kv_ref[here, :HEAD]
    values = kv_ref[here, HEAD:]
    for h in range(8):
        cols = slice(h * HEAD, (h + 1) * HEAD)
        s = mm_nt(q_ref[:, cols], keys) * (SCALE * LOG2E) + bias_ref[...]
        top = jnp.max(s, axis=1, keepdims=True)
        p = jnp.exp2(s - top)
        total = jnp.sum(p, axis=1, keepdims=True)
        mixed_ref[:, cols] = (mm(p.astype(BF), values) / total).astype(BF)
        lse_ref[:, h : h + 1] = top + jnp.log2(total)


def attend(info, q, far, near, own):
    rows = q.shape[0]
    return kernel(
        attend_kernel,
        "attend",
        rows // ROWS,
        (info, q, far, near, own),
        [by_rows(8 * HEAD)] + [None] * 3,
        [by_rows(8 * HEAD), by_rows(8), None],
        [
            out((rows, 8 * HEAD), BF),
            out((rows, 8), F32),
            out((3 * rows, 2 * HEAD), BF),
        ],
        cost(4 * rows * D * SPAN, 5 << 20, rows * 8 * SPAN),
        [pltpu.VMEM((ROWS, SPAN), F32)],
    )


def project_out_kernel(info, *refs):
    mixed_ref, x_ref, gain_ref, w_o = *refs[:3], refs[3:5]
    hidden_ref, normed_ref = refs[5:]
    hidden = x_ref[...].astype(F32)
    for j in range(4):
        mixed = mixed_ref[:, 2 * j * HEAD : 2 * (j + 1) * HEAD]
        hidden = hidden + mm_nt(mixed, two_heads(w_o[j // 2], j % 2))
    hidden_ref[...] = hidden
    inv = lax.rsqrt(jnp.mean(hidden * hidden, axis=1, keepdims=True) + EPSILON)
    normed_ref[...] = (hidden * inv * gain_ref[1:2, :].astype(F32)).astype(BF)


def project_out(info, mixed, x, gains, w_o):
    rows = x.shape[0]
    return kernel(
        project_out_kernel,
        "project_out",
        rows // ROWS,
        (info, mixed, x, gains, *w_o),
        [by_rows(8 * HEAD), by_rows(D)] + [None] * 3,
        [by_rows(D), by_rows(D)],
        [out((rows, D), F32), out((rows, D), BF)],
        cost(2 * rows * D * D, 7 << 20),
    )


def norm_back_kernel(info, *refs):
    own_ref, cot_ref, hidden_ref, gain_ref, *came_refs = refs[:6]
    gh_ref, ghl_ref, gg_ref = refs[6:]

    @pl.when(pl.program_id(0) == 0)
    def _():
        gg_ref[...] = jnp.zeros_like(gg_ref)

    came = jnp.where(pl.program_id(0) == 0, came_refs[0][...], came_refs[1][...])
    grad = own_ref[...].astype(F32) + came.astype(F32)
    hidden = hidden_ref[...]
    inv = lax.rsqrt(jnp.mean(hidden * hidden, axis=1, keepdims=True) + EPSILON)
    hat = hidden * inv
    gg_ref[0:1, :] += jnp.sum(grad * hat, axis=0, keepdims=True)
    g = grad * gain_ref[1:2, :].astype(F32)
    dots = jnp.mean(g * hat, axis=1, keepdims=True)
    grad_hidden = cot_ref[...].astype(F32) + inv * (g - hat * dots)
    gh_ref[...] = grad_hidden
    ghl_ref[...] = grad_hidden.astype(BF)


def norm_back(info, own, came, cot, hidden, gains):
    rows = hidden.shape[0]
    return kernel(
        norm_back_kernel,
        "norm_back",
        rows // ROWS,
        (info, own, cot, hidden, gains, *came),
        [by_rows(D)] * 3 + [None] * 3,
        [by_rows(D), by_rows(D), None],
        [out((rows, D), F32), out((rows, D), BF), out((8, D), F32)],
        cost(20 * rows * D, 10 << 20),
    )


def attend_back_kernel(info, *refs):
    low_ref, cos_ref, sin_ref, q_ref, kv_ref, mixed_ref, lse_ref = refs[:7]
    w_o = refs[7:9]
    gq_ref, far_ref, near_ref, here_ref, gkv_ref, bias_ref, gm_ref, inner_ref, p_ref, gs_ref = refs[9:]
    step = pl.program_id(0)
    rows = here_ref.shape[0]

    @pl.when(step == 0)
    def _():
        gkv_ref[...] = jnp.zeros_like(gkv_ref)

    col = lax.broadcasted_iota(jnp.int32, (SPAN, ROWS), 0)
    row = lax.broadcasted_iota(jnp.int32, (SPAN, ROWS), 1)
    pos = info[ROW_START] - WINDOW + step * ROWS + col
    ahead = col - row - WINDOW
    inside = (ahead <= 0) & (ahead > -WINDOW) & (pos >= 0)
    inside = inside & (pos < info[LENGTHS + info[SLOT]])
    bias_ref[...] = jnp.where(inside | (ahead == 0), 0.0, NEG).astype(F32)

    low = low_ref[...]
    for j in range(4):
        two = mm(low, two_heads(w_o[j // 2], j % 2)).astype(BF)
        gm_ref[:, 2 * j * HEAD : 2 * (j + 1) * HEAD] = two
        for i in range(2):
            h = 2 * j + i
            mixed = mixed_ref[:, h * HEAD : (h + 1) * HEAD].astype(F32)
            gm = two[:, i * HEAD : (i + 1) * HEAD].astype(F32)
            inner_ref[:, h : h + 1] = jnp.sum(gm * mixed, axis=1, keepdims=True)
    inner = inner_ref[...].T
    lse = lse_ref[...].T
    here = pl.ds(step * ROWS, SPAN)
    keys_t = kv_ref[here, :HEAD].T
    for j in range(4):
        for i in range(2):
            h = 2 * j + i
            cols = slice(h * HEAD, (h + 1) * HEAD)
            q, gm = q_ref[:, cols], gm_ref[:, cols]
            for block in range(0, SPAN, ROWS):
                part = slice(block, block + ROWS)
                there = pl.ds(step * ROWS + block, ROWS)
                s = mm_nt(kv_ref[there, :HEAD], q) * (SCALE * LOG2E) + bias_ref[part, :]
                p = jnp.exp2(s - lse[h : h + 1, :])
                gp = mm_nt(kv_ref[there, HEAD:], gm)
                p_ref[part, i * ROWS : (i + 1) * ROWS] = p.astype(BF)
                gs_ref[part, i * ROWS : (i + 1) * ROWS] = (p * (gp - inner[h : h + 1, :])).astype(BF)
            gq = (mm(keys_t, gs_ref[:, i * ROWS : (i + 1) * ROWS]) * SCALE).T
            gq_ref[:, cols] = turn(gq, cos_ref[...], -sin_ref[...]).astype(BF)

        def stacked(ref):
            return jnp.concatenate(
                [ref[:, h * HEAD : (h + 1) * HEAD] for h in (2 * j, 2 * j + 1)], axis=0
            )

        gkv_ref[here, :HEAD] += mm(gs_ref[...], stacked(q_ref))
        gkv_ref[here, HEAD:] += mm(p_ref[...], stacked(gm_ref))

    @pl.when(step == pl.num_programs(0) - 1)
    def _():
        for i, ref in enumerate((far_ref, near_ref, here_ref)):
            block = slice(i * rows, (i + 1) * rows)
            ref[:, :HEAD] = (gkv_ref[block, :HEAD] * SCALE).astype(ref.dtype)
            ref[:, HEAD:] = gkv_ref[block, HEAD:].astype(ref.dtype)


def attend_back(info, low, cosine, sine, q, kv, mixed, lse, w_o):
    rows = q.shape[0]
    wide = by_rows(8 * HEAD)
    return kernel(
        attend_back_kernel,
        "attend_back",
        rows // ROWS,
        (info, low, cosine, sine, q, kv, mixed, lse, *w_o),
        [by_rows(D), by_rows(HEAD), by_rows(HEAD), wide, None, wide, by_rows(8), None, None],
        [wide] + [None] * 3,
        [out((rows, 8 * HEAD), BF)] + [out((rows, 2 * HEAD), k) for k in (BF, BF, F32)],
        cost(10 * rows * D * (SPAN + HEAD), 12 << 20, rows * 8 * SPAN),
        [
            pltpu.VMEM(kv.shape, F32),
            pltpu.VMEM((SPAN, ROWS), F32),
            pltpu.VMEM((ROWS, 8 * HEAD), BF),
            pltpu.VMEM((ROWS, 8), F32),
            pltpu.VMEM((SPAN, 2 * ROWS), BF),
            pltpu.VMEM((SPAN, 2 * ROWS), BF),
        ],
        60 << 20,
    )


def project_back_kernel(info, *refs):
    gq_ref, here_ref, near_ref, far_ref, cos_ref, sin_ref, x_ref, gain_ref, gh_ref = refs[:9]
    wq_own, wq_core, wkv_ref = refs[9:12]
    gkv_ref, gg_ref, *piece_refs = refs[12:18]
    buffer_ref = refs[18]

    @pl.when(pl.program_id(0) == 0)
    def _():
        gg_ref[...] = jnp.zeros_like(gg_ref)

    grad = here_ref[...] + near_ref[...].astype(F32) + far_ref[...].astype(F32)
    gkv_ref[:, :HEAD] = turn(grad[:, :HEAD], cos_ref[...], -sin_ref[...]).astype(BF)
    gkv_ref[:, HEAD:] = grad[:, HEAD:].astype(BF)
    normed_grad = mm_nt(gkv_ref[...], wkv_ref[...])
    for j in range(4):
        weights = two_heads(wq_own if j < 2 else wq_core, j % 2)
        normed_grad = normed_grad + mm_nt(gq_ref[:, 2 * j * HEAD : 2 * (j + 1) * HEAD], weights)
    resid = x_ref[...].astype(F32)
    inv = lax.rsqrt(jnp.mean(resid * resid, axis=1, keepdims=True) + EPSILON)
    hat = resid * inv
    gg_ref[0:1, :] += jnp.sum(normed_grad * hat, axis=0, keepdims=True)
    g = normed_grad * gain_ref[0:1, :].astype(F32)
    dots = jnp.mean(g * hat, axis=1, keepdims=True)
    buffer_ref[...] = gh_ref[...] + inv * (g - hat * dots)
    for k in range(4):
        piece_refs[k][...] = buffer_ref[:, place(info, k)].astype(BF)


def project_back(info, gq, grad_kv, near, far, cosine, sine, x, gains, grad_hidden, w_q, w_kv):
    rows = gq.shape[0]
    steps = rows // ROWS
    pair_rows = by_rows(2 * HEAD)
    return kernel(
        project_back_kernel,
        "project_back",
        steps,
        (info, gq, grad_kv, near, far, cosine, sine, x, gains, grad_hidden, *w_q, w_kv),
        [
            by_rows(8 * HEAD),
            pair_rows,
            pair_rows,
            pair_rows,
            by_rows(HEAD),
            by_rows(HEAD),
            by_rows(D),
            None,
            by_rows(D),
            None,
            None,
            None,
        ],
        [pair_rows, None] + [by_rows(WIDE)] * 4,
        [out((rows, 2 * HEAD), BF), out((8, D), F32)] + [out((rows, WIDE), BF)] * 4,
        cost(2 * rows * D * 10 * HEAD, 10 << 20),
        [pltpu.VMEM((ROWS, D), F32)],
    )


def halves(ref, info, shards, core):
    sub = D // shards // 2
    at_core = info[CORE] ^ core
    return jnp.concatenate(
        [
            ref[:, pl.ds(pl.multiple_of(d * 2 * sub + at_core * sub, HEAD), sub)]
            for d in range(shards)
        ],
        axis=1,
    )


def head_grads_kernel(shards, info, *refs):
    sub = D // shards // 2
    for at_pair in range(2):
        left_ref, right_ref = refs[2 * at_pair : 2 * at_pair + 2]
        for core in range(2):
            mine = halves(left_ref, info, shards, core)
            for j in range(2):
                cols = []
                for k in (2 * j, 2 * j + 1):
                    for kc in (core, 1 - core):
                        cols.append(right_ref[:, (kc * 4 + k) * HEAD : (kc * 4 + k + 1) * HEAD])
                grad = mm_tn(mine, jnp.concatenate(cols, axis=1)).astype(BF)
                for i in range(2):
                    part = grad[:, i * WIDE : (i + 1) * WIDE].reshape(shards, sub, WIDE)
                    refs[4 + core][2 * j + i, :, at_pair * sub : (at_pair + 1) * sub, :] = part


def key_grads_kernel(shards, info, *refs):
    normed_ref, gkv_ref, ga_ref, gm_ref = refs[:4]
    sub = D // shards // 2
    gains = [r[0:1, k * WIDE : (k + 1) * WIDE] for r in (ga_ref, gm_ref) for k in range(4)]
    gains = jnp.concatenate(gains + [jnp.zeros((8, WIDE), F32)], axis=0).astype(BF)
    for core in range(2):
        grad = mm_tn(halves(normed_ref, info, shards, core), gkv_ref[...]).astype(BF)
        for d in range(shards):
            refs[4 + core][d, :sub, :] = grad[d * sub : (d + 1) * sub, :]
            refs[4 + core][d, sub:, :] = gains


def key_grads(info, c, shards, normed, gkv, ga, gm):
    sub = D // shards // 2
    if sub % HEAD:
        keys = mm_tn(normed, gkv).astype(BF).reshape(shards, 2, sub, WIDE)
        gains = jnp.concatenate([ga[0].reshape(4, WIDE), gm[0].reshape(4, WIDE)])
        gains = jnp.concatenate([gains, jnp.zeros((8, WIDE), F32)]).astype(BF)
        gains = jnp.broadcast_to(gains, (shards, 16, WIDE))
        return [jnp.concatenate([at(keys, c ^ core, 1), gains], axis=1) for core in range(2)]
    return kernel(
        functools.partial(key_grads_kernel, shards),
        "key_grads",
        1,
        (info, normed, gkv, ga, gm),
        [None] * 4,
        [None] * 2,
        [out((shards, sub + 16, WIDE), BF)] * 2,
        cost(2 * normed.shape[0] * D * WIDE, 2 << 20),
    )


def head_grads(info, c, shards, pairs):
    rows = pairs[0].shape[0]
    sub = D // shards // 2
    if sub % HEAD:
        parts = [[], []]
        for left, right in (pairs[:2], pairs[2:]):
            grad = mm_tn(left, right).astype(BF).reshape(shards, 2, sub, 2, 4, HEAD)
            for core in range(2):
                mine = at(grad, c ^ core, 1)
                mine = mine[:, :, ::-1] if core else mine
                mine = mine.transpose(3, 0, 1, 2, 4).reshape(4, shards, sub, WIDE)
                parts[core].append(mine)
        return [jnp.concatenate(p, axis=2) for p in parts]
    return kernel(
        functools.partial(head_grads_kernel, shards),
        "head_grads",
        1,
        (info, *pairs),
        [None] * 4,
        [None] * 2,
        [out((4, shards, 2 * sub, WIDE), BF)] * 2,
        cost(4 * rows * D * D, 10 << 20),
    )


def sum_parts_kernel(info, *refs):
    for k in range(4):
        refs[2 + k][...] = (refs[0][k].astype(F32) + refs[1][k].astype(F32)).astype(BF)


def sum_parts(info, mine, other):
    return kernel(
        sum_parts_kernel,
        "sum_parts",
        1,
        (info, mine, other),
        [None] * 2,
        [None] * 4,
        [out(mine.shape[1:], BF)] * 4,
        cost(0, 6 << 20),
    )


def mlp_kernel(units, first, cut_up, info, *refs):
    rows, cot = refs[0][...], refs[1][...]
    weights = refs[2:4]
    active_ref, ggu_ref, branch_ref, *gn_refs = refs[4 if first else 6 :]
    root = math.sqrt(2 / math.pi)
    grad_normed = 0.0 if first else refs[4][...].astype(F32)
    branch = 0.0 if first else refs[5][...].astype(F32)
    for part in range(2):
        w_gu = weights[part][:, : 2 * units]
        w_dt = weights[part][:, 2 * units :]
        lin = mm(rows, w_gu)
        gate, up = lin[:, :units], lin[:, units:]
        grad_active = mm(cot, w_dt)
        square = gate * gate
        tanh = jnp.tanh(root * gate * (1.0 + 0.044715 * square))
        side = 0.5 * (1.0 + tanh)
        gelu = gate * side
        slope = side + gelu * (1.0 - tanh) * (root + 3 * 0.044715 * root * square)
        active = (gelu * up).astype(BF)
        grad_gu = jnp.concatenate(
            [(grad_active * up * slope).astype(BF), (grad_active * gelu).astype(BF)], axis=1
        )
        active_ref[:, part * units : (part + 1) * units] = active
        ggu_ref[:, part * 2 * units : (part + 1) * 2 * units] = grad_gu
        grad_normed = grad_normed + mm_nt(grad_gu, w_gu)
        branch = branch + mm_nt(active, w_dt)
    branch_ref[...] = branch.astype(BF)
    if not cut_up:
        gn_refs[0][...] = grad_normed.astype(BF)
    else:
        for i in range(2):

            @pl.when(pl.program_id(0) == i)
            def _():
                gn_refs[i][...] = grad_normed.astype(BF)


def mlp(info, rows, cot, weights, before=(), cut_up=False):
    count = rows.shape[0]
    units = weights[0].shape[1] // 3
    widths = (2 * units, 4 * units, D)
    outs = [out((count, w), BF) for w in widths]
    outs += [out((ROWS, D), BF)] * 2 if cut_up else [out((count, D), BF)]
    return kernel(
        functools.partial(mlp_kernel, units, not before, cut_up),
        "mlp",
        count // ROWS,
        (info, rows, cot, *weights, *before),
        [by_rows(D)] * 2 + [None] * 2 + [by_rows(D)] * len(before),
        [by_rows(w) for w in widths] + ([None] * 2 if cut_up else [by_rows(D)]),
        outs,
        cost(24 * count * D * units, 14 << 20, count * 2 * units),
    )


def unit_grads_kernel(info, *refs):
    rows_refs, cot_refs, gu_refs, act_refs, out_refs = (refs[i : i + 2] for i in range(0, 10, 2))
    units = act_refs[0].shape[1] // 2
    for part in range(2):
        gu = slice(part * 2 * units, (part + 1) * 2 * units)
        act = slice(part * units, (part + 1) * units)
        up = mm_tn(rows_refs[0][...], gu_refs[0][:, gu]) + mm_tn(rows_refs[1][...], gu_refs[1][:, gu])
        down = mm_tn(cot_refs[0][...], act_refs[0][:, act]) + mm_tn(cot_refs[1][...], act_refs[1][:, act])
        out_refs[part][:, : 2 * units] = up.astype(BF)
        out_refs[part][:, 2 * units :] = down.astype(BF)


def unit_grads(info, rows, cots, grads, actives):
    count = rows[0].shape[0]
    units = actives[0].shape[1] // 2
    columns = pl.BlockSpec((count, WIDE), lambda i, s: (0, i))
    return kernel(
        unit_grads_kernel,
        "unit_grads",
        D // WIDE,
        (info, *rows, *cots, *grads, *actives),
        [columns] * 4 + [None] * 4,
        [pl.BlockSpec((WIDE, 3 * units), lambda i, s: (i, 0))] * 2,
        [out((D, 3 * units), BF)] * 2,
        cost(24 * count * D * units, 14 << 20),
    )


def split_kernel(info, *refs):
    own_ref, hidden_ref, far_ref = refs[:3]
    pieces, buffer_ref = refs[3:7], refs[7]
    for slot in range(2):
        total = own_ref[...].astype(F32) + hidden_ref[...] if slot == 0 else far_ref[...].astype(F32)
        buffer_ref[...] = total
        for k in range(4):
            pieces[k][slot ^ (k >> 1)] = buffer_ref[:, place(info, k)].astype(BF)


def split(info, own, hidden, far):
    rows = own.shape[0]
    return kernel(
        split_kernel,
        "split",
        1,
        (info, own, hidden, far),
        [None] * 3,
        [None] * 4,
        [out((2, rows, WIDE), BF)] * 4,
        cost(0, 8 << 20),
        [pltpu.VMEM((rows, D), F32)],
    )


def swap(value, axis):
    return lax.ppermute(value, axis, [(0, 1), (1, 0)])


def swap_both(value):
    return lax.ppermute(value, ("ty", "tx"), [(i, i ^ 3) for i in range(4)])


def to_next(value, back=False):
    pairs = [(0, 1), (1, 2), (2, 3), (3, 0)]
    return lax.ppermute(value, ("ctx", "tx"), [p[::-1] for p in pairs] if back else pairs)


def exchange(parts):
    return [parts[0], swap(parts[1], "tx"), swap(parts[2], "ty"), swap_both(parts[3])]


def after(value, *others):
    return lax.optimization_barrier((value, others))[0]


def pick(flag, ones, zeros):
    return jnp.where(flag == 1, ones, zeros)


def pair(flag, own, other, axis):
    return jnp.concatenate([pick(flag, other, own), pick(flag, own, other)], axis=axis)


def half_at(value, index, axis):
    size = value.shape[axis] // 2
    return lax.dynamic_slice_in_dim(value, index * size, size, axis)


def at(value, index, axis=0):
    return lax.dynamic_index_in_dim(value, index, axis, False)


def add(*values):
    return sum(v.astype(F32) for v in values)


DIRECT = 4


def to_shard(value, step):
    shards = lax.axis_size("fsdp")
    return lax.ppermute(value, "fsdp", [(i, (i + step) % shards) for i in range(shards)])


def fsdp_gather(part, axis):
    shards = lax.axis_size("fsdp")
    if shards > DIRECT:
        return lax.all_gather(part, "fsdp", axis=axis, tiled=True)
    size = part.shape[axis]
    z = lax.axis_index("fsdp")
    shape = part.shape[:axis] + (shards * size,) + part.shape[axis + 1 :]
    full = lax.dynamic_update_slice_in_dim(jnp.zeros(shape, part.dtype), part, z * size, axis)
    for step in range(1, shards):
        origin = (z - step) % shards
        full = lax.dynamic_update_slice_in_dim(full, to_shard(part, step), origin * size, axis)
    return full


def fsdp_scatter(parts):
    shards = lax.axis_size("fsdp")
    if shards > DIRECT:
        return lax.psum_scatter(parts, "fsdp", scatter_dimension=0, tiled=False).astype(F32)
    z = lax.axis_index("fsdp")
    came = [to_shard(at(parts, (z + step) % shards), step) for step in range(1, shards)]
    return add(at(parts, z), *came)


def fsdp_halve(parts):
    shards = lax.axis_size("fsdp")
    if shards > DIRECT:
        return lax.psum_scatter(parts, "fsdp", scatter_dimension=0, tiled=False)
    z = lax.axis_index("fsdp")
    count = shards // 2
    while count:
        parts = parts.reshape((2, count) + parts.shape[1:])
        side = (z // count) % 2
        came = lax.ppermute(at(parts, 1 - side), "fsdp", [(i, i ^ count) for i in range(shards)])
        parts = add(at(parts, side), came).astype(BF)
        count //= 2
    return parts[0]


def body(
    tokens, lengths, w_query, w_keyval, w_out, w_gateup, w_down, gain_attn, gain_mlp, cotangent
):
    shards = lax.axis_size("fsdp")
    z, c = lax.axis_index("fsdp"), lax.axis_index("ctx")
    y, x = lax.axis_index("ty"), lax.axis_index("tx")
    me = 2 * y + x
    seq_rows = tokens.shape[1]
    rows = seq_rows // 2
    depth = w_query.shape[0]
    sub = depth // 2
    units = w_gateup.shape[2] // 2
    row_start = c * seq_rows + x * rows
    info = jnp.stack(
        [row_start, c, x, me, y, lengths[0], lengths[1]]
    ).astype(jnp.int32)

    *sends, qkv_part, mlp_part = prepare(
        info, tokens, cotangent, gain_attn, gain_mlp, w_query, w_keyval, w_out, w_gateup, w_down
    )

    qkv = fsdp_gather(qkv_part, 1)
    pieces = exchange(sends[:4])
    own_cot, x_cot = sends[4:]
    qkv, mlp_part = after([qkv, mlp_part], pieces)
    w_near = lax.all_gather(mlp_part, "fsdp", axis=0, tiled=True)
    w_q = jnp.stack(exchange([qkv[0]] * 4))
    w_q = [w_q, swap(w_q, "ctx")]
    w_kv = [qkv, swap(qkv[1], "ctx")]
    qkv_late, own_cot, x_cot = after([qkv, own_cot, x_cot], w_q[0])
    cot_x, cot_y = swap(x_cot, "tx"), swap(own_cot, "ty")

    half_width = HEAD // 2
    freq = 10000.0 ** (-jnp.arange(half_width, dtype=F32) / half_width)
    angles = (row_start + jnp.arange(rows, dtype=jnp.int32)).astype(F32)[:, None] * freq[None, :]
    cosine, sine = jnp.cos(angles), jnp.sin(angles)
    cosine = jnp.concatenate([cosine, cosine], axis=1)
    sine = jnp.concatenate([-sine, sine], axis=1)

    x_rows, gain_rows, normed_attn, q, kv_own, w_kv = project(
        info, pieces, w_q, w_kv, cosine, sine
    )
    kv_near, kv_far = to_next(kv_own), swap(kv_own, "ctx")
    w_o = exchange([after(qkv_late[2], kv_own)] * 4)
    q, cot_x, cot_y = after([q, cot_x, cot_y], kv_near)
    cot_both = swap(cot_x, "ty")
    mixed, lse, kv = attend(info, q, kv_far, kv_near, kv_own)
    w_o, w_near, cot_both, mixed = after([w_o, w_near, cot_both, mixed])
    w_o = jnp.stack(w_o)
    w_o = [w_o, swap(w_o, "ctx")]
    w_far = swap(w_near, "tx")
    w_near = [w_near, swap(w_near, "ctx")]
    hidden, normed_mlp = project_out(info, mixed, x_rows, gain_rows, w_o)
    cot_parts = after([own_cot, cot_x, cot_y, cot_both], normed_mlp)
    cots = assemble(info, cot_parts)

    far = swap(normed_mlp, "ty")
    near_act, near_gu, *near_sums = mlp(info, normed_mlp, cots[0], w_near)
    far = after(far, near_act)
    far_act, far_gu, *far_sums = mlp(info, far, cots[1], w_near)
    mlp_rows = [normed_mlp, far]

    def over_cores(grads):
        return add(grads[0], swap(grads[1], "ctx")).astype(BF)

    def over_fsdp(grads):
        return lax.psum_scatter(grads, "fsdp", scatter_dimension=0, tiled=True)

    own_grads = unit_grads(info, mlp_rows, cots, [near_gu, far_gu], [near_act, far_act])
    w_far, own_grads = after([w_far, own_grads])
    w_far = [w_far, swap(w_far, "ctx")]
    own_grads, w_far = after([over_cores(own_grads), w_far])
    own_sums = over_fsdp(own_grads)
    far_act, far_gu, far_branch, *gn_y = mlp(
        info, far, cots[1], w_far, [far_sums[1], far_sums[0]], True
    )
    near_sums = after(near_sums, gn_y)
    gn_y = [swap(g, "ty") for g in gn_y]
    near_act, near_gu, branch, gn = mlp(
        info, normed_mlp, cots[0], w_far, [near_sums[1], near_sums[0]]
    )
    out_parts = split(info, branch, hidden, after(far_branch, gn))
    gn_y[0], near_act = after([gn_y[0], near_act], out_parts)
    other_grads = unit_grads(info, mlp_rows, cots, [near_gu, far_gu], [near_act, far_act])
    gn_y = after(gn_y, other_grads)

    grad_hidden, grad_low, gg_mlp = norm_back(
        info, gn, gn_y, cots[0], hidden, gain_rows
    )

    other_grads, grad_low = after([over_cores(after(other_grads, gn_y)), grad_low])
    other_sums = over_fsdp(other_grads)
    out_came = exchange(after(out_parts, gn_y))
    grad_q, kv_far, kv_near, kv_here = attend_back(
        info, grad_low, cosine, sine, q, kv, mixed, lse, w_o
    )
    kv_near, kv_far = to_next(kv_near, True), swap(kv_far, "ctx")
    grad_q, out_came, own_sums = after([grad_q, out_came, own_sums])
    mine, other = head_grads(
        info, c, shards, after([normed_attn, grad_q, grad_low, mixed], kv_near)
    )
    chip = sum_parts(info, mine, swap(other, "ctx"))
    plane = exchange(chip)
    kv_here = after(kv_here, chip)
    grad_kv, gg_attn, *grad_pieces = project_back(
        info,
        grad_q,
        kv_here,
        kv_near,
        kv_far,
        cosine,
        sine,
        x_rows,
        gain_rows,
        grad_hidden,
        w_q,
        w_kv,
    )
    mine, other = key_grads(info, c, shards, normed_attn, grad_kv, gg_attn, gg_mlp)
    keys = swap(other, "ctx")
    plane, mine = after([plane, mine])
    plane = add(*plane).astype(BF)
    keys, other_sums, grad_pieces = after([keys, other_sums, grad_pieces], plane)
    keys = add(mine, keys).astype(BF)
    total = fsdp_scatter(jnp.concatenate([plane, keys], axis=1))
    grad_came = after(exchange(grad_pieces), total)
    from_x = swap(other_sums, "tx")
    keys = add(*exchange([total[2 * sub :].astype(BF)] * 4))
    total = [pair(c, g[:, :HEAD], g[:, HEAD:], 1) for g in (total[:sub], total[sub : 2 * sub])]
    grad_query, grad_output_proj = total[0], total[1].T
    grad_keyval = keys[:sub]
    gain_sums = [at(keys[sub + 4 * i : sub + 4 * i + 4], me) for i in range(2)]

    came = grad_came
    slot_own = pair(x, came[0], came[1], 0)
    slot_other = pair(x, came[2], came[3], 0)
    grad_tokens = jnp.stack(
        [pick(y, slot_other, slot_own), pick(y, slot_own, slot_other)]
    ).astype(F32)

    halves_out = [add(out_came[0], out_came[2]), add(out_came[1], out_came[3])]
    outputs = pair(x, *(h.astype(BF) for h in halves_out), 1)
    outputs = jnp.stack([pick(y, outputs[1], outputs[0]), pick(y, outputs[0], outputs[1])])

    mlp_grads = add(own_sums, from_x).astype(BF)
    mlp_other = swap(half_at(mlp_grads, 1 - c, 0), "ctx")
    mlp_own = half_at(mlp_grads, c, 0)

    def units_of(i):
        span = slice(i * units, (i + 1) * units)
        return pair(c, mlp_own[:, span], mlp_other[:, span], 1).astype(F32)

    grad_gateup = jnp.stack([units_of(0), units_of(1)])
    grad_down = units_of(2).T

    return (
        outputs,
        grad_tokens,
        grad_query,
        grad_keyval,
        grad_output_proj,
        grad_gateup,
        grad_down,
        gain_sums[0],
        gain_sums[1],
    )


def solution(mesh):
    names = dict(zip(mesh.axis_names, mesh.devices.shape))
    grid = mesh.devices.reshape(names["fsdp"], names["ctx"], 2, names["tp"] // 2)
    split = Mesh(grid, ("fsdp", "ctx", "ty", "tx"))
    tp = ("ty", "tx")
    in_specs = (
        P("fsdp", "ctx", tp),
        P("fsdp"),
        P("fsdp", tp),
        P("fsdp", None),
        P(tp, "fsdp"),
        P(None, "fsdp", tp),
        P(tp, "fsdp"),
        P(tp),
        P(tp),
        P("fsdp", "ctx", tp),
    )
    out_specs = (
        P("fsdp", "ctx", tp),
        P("fsdp", "ctx", tp),
        P(("fsdp", "ctx"), tp),
        P(("fsdp", "ctx"), None),
        P(tp, ("fsdp", "ctx")),
        P(None, ("fsdp", "ctx"), tp),
        P(tp, ("fsdp", "ctx")),
        P(tp),
        P(tp),
    )
    return jax.shard_map(body, mesh=split, in_specs=in_specs, out_specs=out_specs, check_vma=False)
```

```python
import functools
import math

import jax
import jax.numpy as jnp
from jax import lax
from jax.experimental import pallas as pl
from jax.experimental.pallas import tpu as pltpu
from jax.sharding import Mesh
from jax.sharding import PartitionSpec as P

D = 1024
HEAD = 128
WINDOW = 1024
ROWS = 256
SPAN = WINDOW + ROWS
WIDE = 256
EPSILON = 1e-06
NEG = -1e30
LOG2E = math.log2(math.e)
SCALE = HEAD**-0.5
BF = jnp.bfloat16
F32 = jnp.float32
LIMIT = 24 << 20
COST = 1 / 16


def mm(a, b):
    return jnp.dot(a, b, preferred_element_type=F32)


def mm_nt(a, b):
    return lax.dot_general(a, b, (((1,), (1,)), ((), ())), preferred_element_type=F32)


def mm_tn(a, b):
    return lax.dot_general(a, b, (((0,), (0,)), ((), ())), preferred_element_type=F32)


def out(shape, kind):
    return jax.ShapeDtypeStruct(shape, kind)


def cost(flops, nbytes, exps=0):
    flops, nbytes, exps = (int(v * COST) for v in (flops, nbytes, exps))
    return pl.CostEstimate(flops=flops, bytes_accessed=nbytes, transcendentals=exps)


ROW_START, CORE, HALF, ME, SLOT, LENGTHS = 0, 1, 2, 3, 4, 5


def place(info, k):
    return pl.ds(pl.multiple_of((info[ME] ^ k) * WIDE, WIDE), WIDE)


def by_rows(width, rows=ROWS):
    return pl.BlockSpec((rows, width), lambda i, s: (i, 0))


def whole(shape):
    return pl.BlockSpec(shape, lambda i, s: (0,) * len(shape))


def kernel(body, name, grid, args, in_specs, out_specs, outs, work, scratch=(), limit=LIMIT):
    call = pl.pallas_call(
        body,
        grid_spec=pltpu.PrefetchScalarGridSpec(
            num_scalar_prefetch=1,
            grid=(grid,),
            in_specs=[s or whole(a.shape) for s, a in zip(in_specs, args[1:])],
            out_specs=[s or whole(o.shape) for s, o in zip(out_specs, outs)],
            scratch_shapes=scratch,
        ),
        out_shape=outs,
        compiler_params=pltpu.CompilerParams(vmem_limit_bytes=limit),
        cost_estimate=work,
        name=name,
    )
    return call(*args)


def turn(value, cosine, sine):
    return value * cosine + pltpu.roll(value, HEAD // 2, 1) * sine


def prepare_kernel(info, *refs):
    tok_ref, cot_ref, ga_ref, gm_ref, wq_ref, wkv_ref, wo_ref, wgu_ref, wd_ref = refs[:9]
    pieces, cots, qkv_ref, mlp_ref = refs[9:13], refs[13:15], *refs[15:]
    gains = jnp.concatenate(
        [r[...].astype(F32).reshape(1, WIDE) for r in (ga_ref, gm_ref)]
        + [jnp.zeros((14, WIDE), F32)],
        axis=0,
    ).astype(BF)
    rows = tok_ref.shape[1] // 2
    c, x, y = info[CORE], info[HALF], info[SLOT]
    units = wd_ref.shape[0] // 2
    column = pl.ds(pl.multiple_of(c * HEAD, HEAD), HEAD)
    qkv_ref[0] = wq_ref[:, column]
    qkv_ref[1] = wkv_ref[:, column]
    qkv_ref[2] = wo_ref[pl.ds(pl.multiple_of(c * HEAD, HEAD), HEAD), :].T
    for k in range(4):
        half = pl.ds(pl.multiple_of((x ^ (k & 1)) * rows, rows), rows)
        pieces[k][:rows, :] = tok_ref[y ^ (k >> 1), half, :]
        pieces[k][rows:, :] = gains
    for k in range(2):
        half = pl.ds(pl.multiple_of((x ^ k) * rows, rows), rows)
        for slot in range(2):
            time = lax.broadcasted_iota(jnp.int32, (rows, WIDE), 0)
            time = time + info[ROW_START] + ((x ^ k) - x) * rows
            value = cot_ref[y ^ slot, half, :]
            cots[k][slot] = jnp.where(
                time < info[LENGTHS + (y ^ slot)], value.astype(F32), 0.0
            ).astype(BF)
    unit = pl.ds(pl.multiple_of(c * units, HEAD), units)
    mlp_ref[:, :units] = wgu_ref[0, :, unit]
    mlp_ref[:, units : 2 * units] = wgu_ref[1, :, unit]
    mlp_ref[:, 2 * units :] = wd_ref[unit, :].T


def prepare(info, tokens, cotangent, gain_attn, gain_mlp, w_query, w_keyval, w_out, w_gateup, w_down):
    rows = tokens.shape[1] // 2
    depth = w_query.shape[0]
    outs = [out((rows + 16, WIDE), BF)] * 4 + [out((2, rows, WIDE), BF)] * 2
    outs += [
        out((3, depth, HEAD), BF),
        out((depth, 3 * w_down.shape[0] // 2), BF),
    ]
    args = (info, tokens, cotangent, gain_attn, gain_mlp, w_query, w_keyval, w_out, w_gateup, w_down)
    return kernel(
        prepare_kernel, "prepare", 1, args, [None] * 9, [None] * 8, outs, cost(0, 6 << 20), (), 60 << 20
    )


def assemble_kernel(info, *refs):
    for k in range(4):
        for slot in range(2):
            refs[4 + slot][:, place(info, k)] = refs[k][slot ^ (k >> 1)]


def assemble(info, parts):
    rows = parts[0].shape[1]
    return kernel(
        assemble_kernel,
        "assemble",
        1,
        (info, *parts),
        [None] * 4,
        [None] * 2,
        [out((rows, D), BF)] * 2,
        cost(0, 8 << 20),
    )


def project_kernel(info, *refs):
    pieces, (wq_own, wq_core, kv_near, kv_core) = refs[:4], refs[4:8]
    cos_ref, sin_ref, x_ref, gain_ref, normed_ref, q_ref, kv_ref, wkv_ref = refs[8:]
    rows = x_ref.shape[0]
    for k in range(4):
        x_ref[:, place(info, k)] = pieces[k][:rows, :]
        gain_ref[:, place(info, k)] = pieces[k][rows:, :]
    resid = x_ref[...].astype(F32)
    inv = lax.rsqrt(jnp.mean(resid * resid, axis=1, keepdims=True) + EPSILON)
    normed = (resid * inv * gain_ref[0:1, :].astype(F32)).astype(BF)
    normed_ref[...] = normed
    cosine, sine = cos_ref[...], sin_ref[...]
    own_first = info[CORE] == 0
    wkv_ref[:, :HEAD] = jnp.where(own_first, kv_near[1], kv_core[...])
    wkv_ref[:, HEAD:] = jnp.where(own_first, kv_core[...], kv_near[1])
    lin = mm(normed, wkv_ref[...])
    kv_ref[:, :HEAD] = turn(lin[:, :HEAD], cosine, sine).astype(BF)
    kv_ref[:, HEAD:] = lin[:, HEAD:].astype(BF)
    for j in range(4):
        lin = mm(normed, two_heads(wq_own if j < 2 else wq_core, j % 2))
        for i in range(2):
            head = turn(lin[:, i * HEAD : (i + 1) * HEAD], cosine, sine)
            q_ref[:, (2 * j + i) * HEAD : (2 * j + i + 1) * HEAD] = head.astype(BF)


def two_heads(ref, j):
    return jnp.concatenate([ref[2 * j], ref[2 * j + 1]], axis=1)


def project(info, pieces, w_q, w_kv, cosine, sine):
    rows = pieces[0].shape[0] - 16
    return kernel(
        project_kernel,
        "project",
        1,
        (info, *pieces, *w_q, *w_kv, cosine, sine),
        [None] * 10,
        [None] * 6,
        [
            out((rows, D), BF),
            out((16, D), BF),
            out((rows, D), BF),
            out((rows, 8 * HEAD), BF),
            out((rows, 2 * HEAD), BF),
            out((D, 2 * HEAD), BF),
        ],
        cost(2 * rows * D * 10 * HEAD, 8 << 20),
    )


def fill_bias(bias_ref, info, step):
    row = lax.broadcasted_iota(jnp.int32, (ROWS, SPAN), 0)
    col = lax.broadcasted_iota(jnp.int32, (ROWS, SPAN), 1)
    pos = info[ROW_START] - WINDOW + step * ROWS + col
    ahead = col - row - WINDOW
    inside = (ahead <= 0) & (ahead > -WINDOW) & (pos >= 0) & (pos < info[LENGTHS + info[SLOT]])
    bias_ref[...] = jnp.where(inside | (ahead == 0), 0.0, NEG).astype(F32)


def attend_kernel(info, *refs):
    q_ref, far_ref, near_ref, own_ref = refs[:4]
    mixed_ref, lse_ref, kv_ref, bias_ref = refs[4:]
    step = pl.program_id(0)
    rows = own_ref.shape[0]

    @pl.when(step == 0)
    def _():
        kv_ref[:rows, :] = far_ref[...]
        kv_ref[rows : 2 * rows, :] = near_ref[...]
        kv_ref[2 * rows :, :] = own_ref[...]

    fill_bias(bias_ref, info, step)
    here = pl.ds(step * ROWS, SPAN)
    keys = kv_ref[here, :HEAD]
    values = kv_ref[here, HEAD:]
    for h in range(8):
        cols = slice(h * HEAD, (h + 1) * HEAD)
        s = mm_nt(q_ref[:, cols], keys) * (SCALE * LOG2E) + bias_ref[...]
        top = jnp.max(s, axis=1, keepdims=True)
        p = jnp.exp2(s - top)
        total = jnp.sum(p, axis=1, keepdims=True)
        mixed_ref[:, cols] = (mm(p.astype(BF), values) / total).astype(BF)
        lse_ref[:, h : h + 1] = top + jnp.log2(total)


def attend(info, q, far, near, own):
    rows = q.shape[0]
    return kernel(
        attend_kernel,
        "attend",
        rows // ROWS,
        (info, q, far, near, own),
        [by_rows(8 * HEAD)] + [None] * 3,
        [by_rows(8 * HEAD), by_rows(8), None],
        [
            out((rows, 8 * HEAD), BF),
            out((rows, 8), F32),
            out((3 * rows, 2 * HEAD), BF),
        ],
        cost(4 * rows * D * SPAN, 5 << 20, rows * 8 * SPAN),
        [pltpu.VMEM((ROWS, SPAN), F32)],
    )


def project_out_kernel(info, *refs):
    mixed_ref, x_ref, gain_ref, w_o = *refs[:3], refs[3:5]
    hidden_ref, normed_ref = refs[5:]
    hidden = x_ref[...].astype(F32)
    for j in range(4):
        mixed = mixed_ref[:, 2 * j * HEAD : 2 * (j + 1) * HEAD]
        hidden = hidden + mm_nt(mixed, two_heads(w_o[j // 2], j % 2))
    hidden_ref[...] = hidden
    inv = lax.rsqrt(jnp.mean(hidden * hidden, axis=1, keepdims=True) + EPSILON)
    normed_ref[...] = (hidden * inv * gain_ref[1:2, :].astype(F32)).astype(BF)


def project_out(info, mixed, x, gains, w_o):
    rows = x.shape[0]
    return kernel(
        project_out_kernel,
        "project_out",
        rows // ROWS,
        (info, mixed, x, gains, *w_o),
        [by_rows(8 * HEAD), by_rows(D)] + [None] * 3,
        [by_rows(D), by_rows(D)],
        [out((rows, D), F32), out((rows, D), BF)],
        cost(2 * rows * D * D, 7 << 20),
    )


def norm_back_kernel(info, *refs):
    own_ref, cot_ref, hidden_ref, gain_ref, *came_refs = refs[:6]
    gh_ref, ghl_ref, gg_ref = refs[6:]

    @pl.when(pl.program_id(0) == 0)
    def _():
        gg_ref[...] = jnp.zeros_like(gg_ref)

    came = jnp.where(pl.program_id(0) == 0, came_refs[0][...], came_refs[1][...])
    grad = own_ref[...].astype(F32) + came.astype(F32)
    hidden = hidden_ref[...]
    inv = lax.rsqrt(jnp.mean(hidden * hidden, axis=1, keepdims=True) + EPSILON)
    hat = hidden * inv
    gg_ref[0:1, :] += jnp.sum(grad * hat, axis=0, keepdims=True)
    g = grad * gain_ref[1:2, :].astype(F32)
    dots = jnp.mean(g * hat, axis=1, keepdims=True)
    grad_hidden = cot_ref[...].astype(F32) + inv * (g - hat * dots)
    gh_ref[...] = grad_hidden
    ghl_ref[...] = grad_hidden.astype(BF)


def norm_back(info, own, came, cot, hidden, gains):
    rows = hidden.shape[0]
    return kernel(
        norm_back_kernel,
        "norm_back",
        rows // ROWS,
        (info, own, cot, hidden, gains, *came),
        [by_rows(D)] * 3 + [None] * 3,
        [by_rows(D), by_rows(D), None],
        [out((rows, D), F32), out((rows, D), BF), out((8, D), F32)],
        cost(20 * rows * D, 10 << 20),
    )


def attend_back_kernel(info, *refs):
    low_ref, cos_ref, sin_ref, q_ref, kv_ref, mixed_ref, lse_ref = refs[:7]
    w_o = refs[7:9]
    gq_ref, far_ref, near_ref, here_ref, gkv_ref, bias_ref, gm_ref, inner_ref, p_ref, gs_ref = refs[9:]
    step = pl.program_id(0)
    rows = here_ref.shape[0]

    @pl.when(step == 0)
    def _():
        gkv_ref[...] = jnp.zeros_like(gkv_ref)

    col = lax.broadcasted_iota(jnp.int32, (SPAN, ROWS), 0)
    row = lax.broadcasted_iota(jnp.int32, (SPAN, ROWS), 1)
    pos = info[ROW_START] - WINDOW + step * ROWS + col
    ahead = col - row - WINDOW
    inside = (ahead <= 0) & (ahead > -WINDOW) & (pos >= 0)
    inside = inside & (pos < info[LENGTHS + info[SLOT]])
    bias_ref[...] = jnp.where(inside | (ahead == 0), 0.0, NEG).astype(F32)

    low = low_ref[...]
    for j in range(4):
        two = mm(low, two_heads(w_o[j // 2], j % 2)).astype(BF)
        gm_ref[:, 2 * j * HEAD : 2 * (j + 1) * HEAD] = two
        for i in range(2):
            h = 2 * j + i
            mixed = mixed_ref[:, h * HEAD : (h + 1) * HEAD].astype(F32)
            gm = two[:, i * HEAD : (i + 1) * HEAD].astype(F32)
            inner_ref[:, h : h + 1] = jnp.sum(gm * mixed, axis=1, keepdims=True)
    inner = inner_ref[...].T
    lse = lse_ref[...].T
    here = pl.ds(step * ROWS, SPAN)
    keys_t = kv_ref[here, :HEAD].T
    for j in range(4):
        for i in range(2):
            h = 2 * j + i
            cols = slice(h * HEAD, (h + 1) * HEAD)
            q, gm = q_ref[:, cols], gm_ref[:, cols]
            for block in range(0, SPAN, ROWS):
                part = slice(block, block + ROWS)
                there = pl.ds(step * ROWS + block, ROWS)
                s = mm_nt(kv_ref[there, :HEAD], q) * (SCALE * LOG2E) + bias_ref[part, :]
                p = jnp.exp2(s - lse[h : h + 1, :])
                gp = mm_nt(kv_ref[there, HEAD:], gm)
                p_ref[part, i * ROWS : (i + 1) * ROWS] = p.astype(BF)
                gs_ref[part, i * ROWS : (i + 1) * ROWS] = (p * (gp - inner[h : h + 1, :])).astype(BF)
            gq = (mm(keys_t, gs_ref[:, i * ROWS : (i + 1) * ROWS]) * SCALE).T
            gq_ref[:, cols] = turn(gq, cos_ref[...], -sin_ref[...]).astype(BF)

        def stacked(ref):
            return jnp.concatenate(
                [ref[:, h * HEAD : (h + 1) * HEAD] for h in (2 * j, 2 * j + 1)], axis=0
            )

        gkv_ref[here, :HEAD] += mm(gs_ref[...], stacked(q_ref))
        gkv_ref[here, HEAD:] += mm(p_ref[...], stacked(gm_ref))

    @pl.when(step == pl.num_programs(0) - 1)
    def _():
        for i, ref in enumerate((far_ref, near_ref, here_ref)):
            block = slice(i * rows, (i + 1) * rows)
            ref[:, :HEAD] = (gkv_ref[block, :HEAD] * SCALE).astype(ref.dtype)
            ref[:, HEAD:] = gkv_ref[block, HEAD:].astype(ref.dtype)


def attend_back(info, low, cosine, sine, q, kv, mixed, lse, w_o):
    rows = q.shape[0]
    wide = by_rows(8 * HEAD)
    return kernel(
        attend_back_kernel,
        "attend_back",
        rows // ROWS,
        (info, low, cosine, sine, q, kv, mixed, lse, *w_o),
        [by_rows(D), by_rows(HEAD), by_rows(HEAD), wide, None, wide, by_rows(8), None, None],
        [wide] + [None] * 3,
        [out((rows, 8 * HEAD), BF)] + [out((rows, 2 * HEAD), k) for k in (BF, BF, F32)],
        cost(10 * rows * D * (SPAN + HEAD), 12 << 20, rows * 8 * SPAN),
        [
            pltpu.VMEM(kv.shape, F32),
            pltpu.VMEM((SPAN, ROWS), F32),
            pltpu.VMEM((ROWS, 8 * HEAD), BF),
            pltpu.VMEM((ROWS, 8), F32),
            pltpu.VMEM((SPAN, 2 * ROWS), BF),
            pltpu.VMEM((SPAN, 2 * ROWS), BF),
        ],
        60 << 20,
    )


def project_back_kernel(info, *refs):
    gq_ref, here_ref, near_ref, far_ref, cos_ref, sin_ref, x_ref, gain_ref, gh_ref = refs[:9]
    wq_own, wq_core, wkv_ref = refs[9:12]
    gkv_ref, gg_ref, *piece_refs = refs[12:18]
    buffer_ref = refs[18]

    @pl.when(pl.program_id(0) == 0)
    def _():
        gg_ref[...] = jnp.zeros_like(gg_ref)

    grad = here_ref[...] + near_ref[...].astype(F32) + far_ref[...].astype(F32)
    gkv_ref[:, :HEAD] = turn(grad[:, :HEAD], cos_ref[...], -sin_ref[...]).astype(BF)
    gkv_ref[:, HEAD:] = grad[:, HEAD:].astype(BF)
    normed_grad = mm_nt(gkv_ref[...], wkv_ref[...])
    for j in range(4):
        weights = two_heads(wq_own if j < 2 else wq_core, j % 2)
        normed_grad = normed_grad + mm_nt(gq_ref[:, 2 * j * HEAD : 2 * (j + 1) * HEAD], weights)
    resid = x_ref[...].astype(F32)
    inv = lax.rsqrt(jnp.mean(resid * resid, axis=1, keepdims=True) + EPSILON)
    hat = resid * inv
    gg_ref[0:1, :] += jnp.sum(normed_grad * hat, axis=0, keepdims=True)
    g = normed_grad * gain_ref[0:1, :].astype(F32)
    dots = jnp.mean(g * hat, axis=1, keepdims=True)
    buffer_ref[...] = gh_ref[...] + inv * (g - hat * dots)
    for k in range(4):
        piece_refs[k][...] = buffer_ref[:, place(info, k)].astype(BF)


def project_back(info, gq, grad_kv, near, far, cosine, sine, x, gains, grad_hidden, w_q, w_kv):
    rows = gq.shape[0]
    steps = rows // ROWS
    pair_rows = by_rows(2 * HEAD)
    return kernel(
        project_back_kernel,
        "project_back",
        steps,
        (info, gq, grad_kv, near, far, cosine, sine, x, gains, grad_hidden, *w_q, w_kv),
        [
            by_rows(8 * HEAD),
            pair_rows,
            pair_rows,
            pair_rows,
            by_rows(HEAD),
            by_rows(HEAD),
            by_rows(D),
            None,
            by_rows(D),
            None,
            None,
            None,
        ],
        [pair_rows, None] + [by_rows(WIDE)] * 4,
        [out((rows, 2 * HEAD), BF), out((8, D), F32)] + [out((rows, WIDE), BF)] * 4,
        cost(2 * rows * D * 10 * HEAD, 10 << 20),
        [pltpu.VMEM((ROWS, D), F32)],
    )


def halves(ref, info, shards, core):
    sub = D // shards // 2
    at_core = info[CORE] ^ core
    return jnp.concatenate(
        [
            ref[:, pl.ds(pl.multiple_of(d * 2 * sub + at_core * sub, HEAD), sub)]
            for d in range(shards)
        ],
        axis=1,
    )


def head_grads_kernel(shards, info, *refs):
    sub = D // shards // 2
    for at_pair in range(2):
        left_ref, right_ref = refs[2 * at_pair : 2 * at_pair + 2]
        for core in range(2):
            mine = halves(left_ref, info, shards, core)
            for j in range(2):
                cols = []
                for k in (2 * j, 2 * j + 1):
                    for kc in (core, 1 - core):
                        cols.append(right_ref[:, (kc * 4 + k) * HEAD : (kc * 4 + k + 1) * HEAD])
                grad = mm_tn(mine, jnp.concatenate(cols, axis=1)).astype(BF)
                for i in range(2):
                    part = grad[:, i * WIDE : (i + 1) * WIDE].reshape(shards, sub, WIDE)
                    refs[4 + core][2 * j + i, :, at_pair * sub : (at_pair + 1) * sub, :] = part


def key_grads_kernel(shards, info, *refs):
    normed_ref, gkv_ref, ga_ref, gm_ref = refs[:4]
    sub = D // shards // 2
    gains = [r[0:1, k * WIDE : (k + 1) * WIDE] for r in (ga_ref, gm_ref) for k in range(4)]
    gains = jnp.concatenate(gains + [jnp.zeros((8, WIDE), F32)], axis=0).astype(BF)
    for core in range(2):
        grad = mm_tn(halves(normed_ref, info, shards, core), gkv_ref[...]).astype(BF)
        for d in range(shards):
            refs[4 + core][d, :sub, :] = grad[d * sub : (d + 1) * sub, :]
            refs[4 + core][d, sub:, :] = gains


def key_grads(info, c, shards, normed, gkv, ga, gm):
    sub = D // shards // 2
    if sub % HEAD:
        keys = mm_tn(normed, gkv).astype(BF).reshape(shards, 2, sub, WIDE)
        gains = jnp.concatenate([ga[0].reshape(4, WIDE), gm[0].reshape(4, WIDE)])
        gains = jnp.concatenate([gains, jnp.zeros((8, WIDE), F32)]).astype(BF)
        gains = jnp.broadcast_to(gains, (shards, 16, WIDE))
        return [jnp.concatenate([at(keys, c ^ core, 1), gains], axis=1) for core in range(2)]
    return kernel(
        functools.partial(key_grads_kernel, shards),
        "key_grads",
        1,
        (info, normed, gkv, ga, gm),
        [None] * 4,
        [None] * 2,
        [out((shards, sub + 16, WIDE), BF)] * 2,
        cost(2 * normed.shape[0] * D * WIDE, 2 << 20),
    )


def head_grads(info, c, shards, pairs):
    rows = pairs[0].shape[0]
    sub = D // shards // 2
    if sub % HEAD:
        parts = [[], []]
        for left, right in (pairs[:2], pairs[2:]):
            grad = mm_tn(left, right).astype(BF).reshape(shards, 2, sub, 2, 4, HEAD)
            for core in range(2):
                mine = at(grad, c ^ core, 1)
                mine = mine[:, :, ::-1] if core else mine
                mine = mine.transpose(3, 0, 1, 2, 4).reshape(4, shards, sub, WIDE)
                parts[core].append(mine)
        return [jnp.concatenate(p, axis=2) for p in parts]
    return kernel(
        functools.partial(head_grads_kernel, shards),
        "head_grads",
        1,
        (info, *pairs),
        [None] * 4,
        [None] * 2,
        [out((4, shards, 2 * sub, WIDE), BF)] * 2,
        cost(4 * rows * D * D, 10 << 20),
    )


def sum_parts_kernel(info, *refs):
    for k in range(4):
        refs[2 + k][...] = (refs[0][k].astype(F32) + refs[1][k].astype(F32)).astype(BF)


def sum_parts(info, mine, other):
    return kernel(
        sum_parts_kernel,
        "sum_parts",
        1,
        (info, mine, other),
        [None] * 2,
        [None] * 4,
        [out(mine.shape[1:], BF)] * 4,
        cost(0, 6 << 20),
    )


def mlp_kernel(units, first, cut_up, info, *refs):
    rows, cot = refs[0][...], refs[1][...]
    weights = refs[2:4]
    active_ref, ggu_ref, branch_ref, *gn_refs = refs[4 if first else 6 :]
    root = math.sqrt(2 / math.pi)
    grad_normed = 0.0 if first else refs[4][...].astype(F32)
    branch = 0.0 if first else refs[5][...].astype(F32)
    for part in range(2):
        w_gu = weights[part][:, : 2 * units]
        w_dt = weights[part][:, 2 * units :]
        lin = mm(rows, w_gu)
        gate, up = lin[:, :units], lin[:, units:]
        grad_active = mm(cot, w_dt)
        square = gate * gate
        tanh = jnp.tanh(root * gate * (1.0 + 0.044715 * square))
        side = 0.5 * (1.0 + tanh)
        gelu = gate * side
        slope = side + gelu * (1.0 - tanh) * (root + 3 * 0.044715 * root * square)
        active = (gelu * up).astype(BF)
        grad_gu = jnp.concatenate(
            [(grad_active * up * slope).astype(BF), (grad_active * gelu).astype(BF)], axis=1
        )
        active_ref[:, part * units : (part + 1) * units] = active
        ggu_ref[:, part * 2 * units : (part + 1) * 2 * units] = grad_gu
        grad_normed = grad_normed + mm_nt(grad_gu, w_gu)
        branch = branch + mm_nt(active, w_dt)
    branch_ref[...] = branch.astype(BF)
    if not cut_up:
        gn_refs[0][...] = grad_normed.astype(BF)
    else:
        for i in range(2):

            @pl.when(pl.program_id(0) == i)
            def _():
                gn_refs[i][...] = grad_normed.astype(BF)


def mlp(info, rows, cot, weights, before=(), cut_up=False):
    count = rows.shape[0]
    units = weights[0].shape[1] // 3
    widths = (2 * units, 4 * units, D)
    outs = [out((count, w), BF) for w in widths]
    outs += [out((ROWS, D), BF)] * 2 if cut_up else [out((count, D), BF)]
    return kernel(
        functools.partial(mlp_kernel, units, not before, cut_up),
        "mlp",
        count // ROWS,
        (info, rows, cot, *weights, *before),
        [by_rows(D)] * 2 + [None] * 2 + [by_rows(D)] * len(before),
        [by_rows(w) for w in widths] + ([None] * 2 if cut_up else [by_rows(D)]),
        outs,
        cost(24 * count * D * units, 14 << 20, count * 2 * units),
    )


def unit_grads_kernel(info, *refs):
    rows_refs, cot_refs, gu_refs, act_refs, out_refs = (refs[i : i + 2] for i in range(0, 10, 2))
    units = act_refs[0].shape[1] // 2
    for part in range(2):
        gu = slice(part * 2 * units, (part + 1) * 2 * units)
        act = slice(part * units, (part + 1) * units)
        up = mm_tn(rows_refs[0][...], gu_refs[0][:, gu]) + mm_tn(rows_refs[1][...], gu_refs[1][:, gu])
        down = mm_tn(cot_refs[0][...], act_refs[0][:, act]) + mm_tn(cot_refs[1][...], act_refs[1][:, act])
        out_refs[part][:, : 2 * units] = up.astype(BF)
        out_refs[part][:, 2 * units :] = down.astype(BF)


def unit_grads(info, rows, cots, grads, actives):
    count = rows[0].shape[0]
    units = actives[0].shape[1] // 2
    columns = pl.BlockSpec((count, WIDE), lambda i, s: (0, i))
    return kernel(
        unit_grads_kernel,
        "unit_grads",
        D // WIDE,
        (info, *rows, *cots, *grads, *actives),
        [columns] * 4 + [None] * 4,
        [pl.BlockSpec((WIDE, 3 * units), lambda i, s: (i, 0))] * 2,
        [out((D, 3 * units), BF)] * 2,
        cost(24 * count * D * units, 14 << 20),
    )


def split_kernel(info, *refs):
    own_ref, hidden_ref, far_ref = refs[:3]
    pieces, buffer_ref = refs[3:7], refs[7]
    for slot in range(2):
        total = own_ref[...].astype(F32) + hidden_ref[...] if slot == 0 else far_ref[...].astype(F32)
        buffer_ref[...] = total
        for k in range(4):
            pieces[k][slot ^ (k >> 1)] = buffer_ref[:, place(info, k)].astype(BF)


def split(info, own, hidden, far):
    rows = own.shape[0]
    return kernel(
        split_kernel,
        "split",
        1,
        (info, own, hidden, far),
        [None] * 3,
        [None] * 4,
        [out((2, rows, WIDE), BF)] * 4,
        cost(0, 8 << 20),
        [pltpu.VMEM((rows, D), F32)],
    )


def swap(value, axis):
    return lax.ppermute(value, axis, [(0, 1), (1, 0)])


def swap_both(value):
    return lax.ppermute(value, ("ty", "tx"), [(i, i ^ 3) for i in range(4)])


def to_next(value, back=False):
    pairs = [(0, 1), (1, 2), (2, 3), (3, 0)]
    return lax.ppermute(value, ("ctx", "tx"), [p[::-1] for p in pairs] if back else pairs)


def exchange(parts):
    return [parts[0], swap(parts[1], "tx"), swap(parts[2], "ty"), swap_both(parts[3])]


def after(value, *others):
    return lax.optimization_barrier((value, others))[0]


def pick(flag, ones, zeros):
    return jnp.where(flag == 1, ones, zeros)


def pair(flag, own, other, axis):
    return jnp.concatenate([pick(flag, other, own), pick(flag, own, other)], axis=axis)


def half_at(value, index, axis):
    size = value.shape[axis] // 2
    return lax.dynamic_slice_in_dim(value, index * size, size, axis)


def at(value, index, axis=0):
    return lax.dynamic_index_in_dim(value, index, axis, False)


def add(*values):
    return sum(v.astype(F32) for v in values)


DIRECT = 4


def to_shard(value, step):
    shards = lax.axis_size("fsdp")
    return lax.ppermute(value, "fsdp", [(i, (i + step) % shards) for i in range(shards)])


def fsdp_gather(part, axis):
    shards = lax.axis_size("fsdp")
    if shards > DIRECT:
        return lax.all_gather(part, "fsdp", axis=axis, tiled=True)
    size = part.shape[axis]
    z = lax.axis_index("fsdp")
    shape = part.shape[:axis] + (shards * size,) + part.shape[axis + 1 :]
    full = lax.dynamic_update_slice_in_dim(jnp.zeros(shape, part.dtype), part, z * size, axis)
    for step in range(1, shards):
        origin = (z - step) % shards
        full = lax.dynamic_update_slice_in_dim(full, to_shard(part, step), origin * size, axis)
    return full


def fsdp_scatter(parts):
    shards = lax.axis_size("fsdp")
    if shards > DIRECT:
        return lax.psum_scatter(parts, "fsdp", scatter_dimension=0, tiled=False).astype(F32)
    z = lax.axis_index("fsdp")
    came = [to_shard(at(parts, (z + step) % shards), step) for step in range(1, shards)]
    return add(at(parts, z), *came)


def fsdp_halve(parts):
    shards = lax.axis_size("fsdp")
    if shards > DIRECT:
        return lax.psum_scatter(parts, "fsdp", scatter_dimension=0, tiled=False)
    z = lax.axis_index("fsdp")
    count = shards // 2
    while count:
        parts = parts.reshape((2, count) + parts.shape[1:])
        side = (z // count) % 2
        came = lax.ppermute(at(parts, 1 - side), "fsdp", [(i, i ^ count) for i in range(shards)])
        parts = add(at(parts, side), came).astype(BF)
        count //= 2
    return parts[0]


def body(
    tokens, lengths, w_query, w_keyval, w_out, w_gateup, w_down, gain_attn, gain_mlp, cotangent
):
    shards = lax.axis_size("fsdp")
    z, c = lax.axis_index("fsdp"), lax.axis_index("ctx")
    y, x = lax.axis_index("ty"), lax.axis_index("tx")
    me = 2 * y + x
    seq_rows = tokens.shape[1]
    rows = seq_rows // 2
    depth = w_query.shape[0]
    sub = depth // 2
    units = w_gateup.shape[2] // 2
    row_start = c * seq_rows + x * rows
    info = jnp.stack(
        [row_start, c, x, me, y, lengths[0], lengths[1]]
    ).astype(jnp.int32)

    *sends, qkv_part, mlp_part = prepare(
        info, tokens, cotangent, gain_attn, gain_mlp, w_query, w_keyval, w_out, w_gateup, w_down
    )

    qkv = fsdp_gather(qkv_part, 1)
    pieces = exchange(sends[:4])
    own_cot, x_cot = sends[4:]
    qkv, mlp_part = after([qkv, mlp_part], pieces)
    w_near = lax.all_gather(mlp_part, "fsdp", axis=0, tiled=True)
    w_q = jnp.stack(exchange([qkv[0]] * 4))
    w_q = [w_q, swap(w_q, "ctx")]
    w_kv = [qkv, swap(qkv[1], "ctx")]
    qkv_late, own_cot, x_cot = after([qkv, own_cot, x_cot], w_q[0])
    cot_x, cot_y = swap(x_cot, "tx"), swap(own_cot, "ty")

    half_width = HEAD // 2
    freq = 10000.0 ** (-jnp.arange(half_width, dtype=F32) / half_width)
    angles = (row_start + jnp.arange(rows, dtype=jnp.int32)).astype(F32)[:, None] * freq[None, :]
    cosine, sine = jnp.cos(angles), jnp.sin(angles)
    cosine = jnp.concatenate([cosine, cosine], axis=1)
    sine = jnp.concatenate([-sine, sine], axis=1)

    x_rows, gain_rows, normed_attn, q, kv_own, w_kv = project(
        info, pieces, w_q, w_kv, cosine, sine
    )
    kv_near, kv_far = to_next(kv_own), swap(kv_own, "ctx")
    w_o = exchange([after(qkv_late[2], kv_own)] * 4)
    q, cot_x, cot_y = after([q, cot_x, cot_y], kv_near)
    cot_both = swap(cot_x, "ty")
    mixed, lse, kv = attend(info, q, kv_far, kv_near, kv_own)
    w_o, w_near, cot_both, mixed = after([w_o, w_near, cot_both, mixed])
    w_o = jnp.stack(w_o)
    w_o = [w_o, swap(w_o, "ctx")]
    w_far = swap(w_near, "tx")
    w_near = [w_near, swap(w_near, "ctx")]
    hidden, normed_mlp = project_out(info, mixed, x_rows, gain_rows, w_o)
    cot_parts = after([own_cot, cot_x, cot_y, cot_both], normed_mlp)
    cots = assemble(info, cot_parts)

    far = swap(normed_mlp, "ty")
    near_act, near_gu, *near_sums = mlp(info, normed_mlp, cots[0], w_near)
    far = after(far, near_act)
    far_act, far_gu, *far_sums = mlp(info, far, cots[1], w_near)
    mlp_rows = [normed_mlp, far]

    def over_cores(grads):
        return add(grads[0], swap(grads[1], "ctx")).astype(BF)

    def over_fsdp(grads):
        return lax.psum_scatter(grads, "fsdp", scatter_dimension=0, tiled=True)

    own_grads = unit_grads(info, mlp_rows, cots, [near_gu, far_gu], [near_act, far_act])
    w_far, own_grads = after([w_far, own_grads])
    w_far = [w_far, swap(w_far, "ctx")]
    own_grads = over_cores(own_grads)
    w_far = after(w_far, own_grads)
    own_sums = over_fsdp(own_grads)
    far_act, far_gu, far_branch, *gn_y = mlp(
        info, far, cots[1], w_far, [far_sums[1], far_sums[0]], True
    )
    near_sums = after(near_sums, gn_y)
    gn_y = [swap(g, "ty") for g in gn_y]
    near_act, near_gu, branch, gn = mlp(
        info, normed_mlp, cots[0], w_far, [near_sums[1], near_sums[0]]
    )
    out_parts = split(info, branch, hidden, after(far_branch, gn))
    gn_y[0], near_act = after([gn_y[0], near_act], out_parts)
    other_grads = unit_grads(info, mlp_rows, cots, [near_gu, far_gu], [near_act, far_act])
    gn_y = after(gn_y, other_grads)

    grad_hidden, grad_low, gg_mlp = norm_back(
        info, gn, gn_y, cots[0], hidden, gain_rows
    )

    other_grads, grad_low = after([over_cores(after(other_grads, gn_y)), grad_low])
    other_sums = over_fsdp(other_grads)
    out_came = exchange(after(out_parts, gn_y))
    grad_q, kv_far, kv_near, kv_here = attend_back(
        info, grad_low, cosine, sine, q, kv, mixed, lse, w_o
    )
    kv_near, kv_far = to_next(kv_near, True), swap(kv_far, "ctx")
    grad_q, own_sums = after([grad_q, own_sums])
    head_inputs = after([normed_attn, grad_q, grad_low, mixed], kv_near, kv_far)
    mine, other = head_grads(info, c, shards, head_inputs)
    out_came = after(out_came, mine)
    chip = sum_parts(info, mine, swap(after(other, out_came), "ctx"))
    plane = exchange(chip)
    kv_here = after(kv_here, chip)
    grad_kv, gg_attn, *grad_pieces = project_back(
        info,
        grad_q,
        kv_here,
        kv_near,
        kv_far,
        cosine,
        sine,
        x_rows,
        gain_rows,
        grad_hidden,
        w_q,
        w_kv,
    )
    mine, other = key_grads(info, c, shards, normed_attn, grad_kv, gg_attn, gg_mlp)
    keys = swap(other, "ctx")
    plane, mine = after([plane, mine])
    plane = add(*plane).astype(BF)
    keys, other_sums, grad_pieces = after([keys, other_sums, grad_pieces], plane)
    keys = add(mine, keys).astype(BF)
    total = fsdp_scatter(jnp.concatenate([plane, keys], axis=1))
    grad_came = after(exchange(grad_pieces), total)
    from_x = swap(other_sums, "tx")
    keys = add(*exchange([total[2 * sub :].astype(BF)] * 4))
    total = [pair(c, g[:, :HEAD], g[:, HEAD:], 1) for g in (total[:sub], total[sub : 2 * sub])]
    grad_query, grad_output_proj = total[0], total[1].T
    grad_keyval = keys[:sub]
    gain_sums = [at(keys[sub + 4 * i : sub + 4 * i + 4], me) for i in range(2)]

    came = grad_came
    slot_own = pair(x, came[0], came[1], 0)
    slot_other = pair(x, came[2], came[3], 0)
    grad_tokens = jnp.stack(
        [pick(y, slot_other, slot_own), pick(y, slot_own, slot_other)]
    ).astype(F32)

    halves_out = [add(out_came[0], out_came[2]), add(out_came[1], out_came[3])]
    outputs = pair(x, *(h.astype(BF) for h in halves_out), 1)
    outputs = jnp.stack([pick(y, outputs[1], outputs[0]), pick(y, outputs[0], outputs[1])])

    mlp_grads = add(own_sums, from_x).astype(BF)
    mlp_other = swap(half_at(mlp_grads, 1 - c, 0), "ctx")
    mlp_own = half_at(mlp_grads, c, 0)

    def units_of(i):
        span = slice(i * units, (i + 1) * units)
        return pair(c, mlp_own[:, span], mlp_other[:, span], 1).astype(F32)

    grad_gateup = jnp.stack([units_of(0), units_of(1)])
    grad_down = units_of(2).T

    return (
        outputs,
        grad_tokens,
        grad_query,
        grad_keyval,
        grad_output_proj,
        grad_gateup,
        grad_down,
        gain_sums[0],
        gain_sums[1],
    )


def solution(mesh):
    names = dict(zip(mesh.axis_names, mesh.devices.shape))
    grid = mesh.devices.reshape(names["fsdp"], names["ctx"], 2, names["tp"] // 2)
    split = Mesh(grid, ("fsdp", "ctx", "ty", "tx"))
    tp = ("ty", "tx")
    in_specs = (
        P("fsdp", "ctx", tp),
        P("fsdp"),
        P("fsdp", tp),
        P("fsdp", None),
        P(tp, "fsdp"),
        P(None, "fsdp", tp),
        P(tp, "fsdp"),
        P(tp),
        P(tp),
        P("fsdp", "ctx", tp),
    )
    out_specs = (
        P("fsdp", "ctx", tp),
        P("fsdp", "ctx", tp),
        P(("fsdp", "ctx"), tp),
        P(("fsdp", "ctx"), None),
        P(tp, ("fsdp", "ctx")),
        P(None, ("fsdp", "ctx"), tp),
        P(tp, ("fsdp", "ctx")),
        P(tp),
        P(tp),
    )
    return jax.shard_map(body, mesh=split, in_specs=in_specs, out_specs=out_specs, check_vma=False)
```
